512 devices in a mesh: ctx: 16 (over z_hi, x, core), head: 32 (over y, z_lo).
Axes of the slice: x: 4, y: 4, z: 16 (z_hi: 2, z_lo: 8; z = z_hi * 8 + z_lo), core: 2. Of those that a mesh axis runs over, the one named last changes fastest.
Arguments:
- query_rows: bfloat16 [32768, 4096], P('ctx', 'head'), may hold values from -6 to 6
- key_rows: bfloat16 [32768, 512], P(('ctx', 'head')), may hold values from -4 to 4
- value_rows: bfloat16 [32768, 512], P(('ctx', 'head')), may hold values from -6 to 6
- selection: int32 [16, 3], replicated, may hold values from -1 to 15, as said below
Outputs:
- attended: bfloat16 [32768, 4096], P('ctx', 'head')
The draws below stay inside these ranges and needn't reach their ends.
Inputs may be any that keep to these rules, and one draw needn't show every extreme that they name: `selection`: row b names block b first, then up to two different earlier blocks; -1 fills a slot that has no earlier block to name, which happens only in rows 0 and 1.
All inputs are finite; a program needn't handle non-finite values.
Results may differ from the reference program's by a relative error of at most 0.0044.
Values may be sent and summed in bfloat16 or wider, within the bound.
A program may use at most 64 MiB of HBM per device.

```python
import jax
import jax.numpy as jnp
from jax import lax

HQ = 32
HK = 4
DH = 128
BLOCK = 2048
SLOTS = 3
NB = 16
TOKENS = 32768


def draw_query_rows(key, part):
    key = jax.random.fold_in(key, 11)
    shape = (TOKENS, HQ * DH)
    return jnp.clip(jax.random.normal(key, shape, jnp.float32), -4.0, 4.0).astype(jnp.bfloat16)


def draw_key_rows(key, part):
    key = jax.random.fold_in(key, 13)
    shape = (TOKENS, HK * DH)
    return jnp.clip(jax.random.normal(key, shape, jnp.float32), -4.0, 4.0).astype(jnp.bfloat16)


def draw_selection(key, part):
    key = jax.random.fold_in(key, 17)
    rows = jnp.arange(NB, dtype=jnp.int32)[:, None]
    cols = jnp.arange(NB, dtype=jnp.int32)[None, :]
    raw = jax.random.randint(key, (NB, NB), 0, 4096) // (cols // 2 + 1)
    ranked = raw * NB + (NB - 1 - cols)
    ranked = jnp.where(cols < rows, ranked, -1)
    picks = jax.lax.top_k(ranked, 2)[1].astype(jnp.int32)
    first = jnp.where(rows[:, 0] >= 1, picks[:, 0], -1)
    second = jnp.where(rows[:, 0] >= 2, picks[:, 1], -1)
    return jnp.stack([rows[:, 0], first, second], axis=1).astype(jnp.int32)


def block_scale(key, shape, cuts, least, high):
    def one(axis_at, blocks):
        draws = jax.random.uniform(jax.random.fold_in(jax.random.fold_in(key, 6), axis_at), (blocks,), jnp.float32, least / len(cuts), high / len(cuts))
        return jnp.repeat(jnp.exp(draws), shape[axis_at] // blocks).reshape((-1,) + (1,) * (len(shape) - axis_at - 1))

    level = one(*cuts[0])
    for cut in cuts[1:]:
        level = level * one(*cut)
    return level


def scatter_about(stream_key, extent, spread, most, shards=(), held_as=jnp.bfloat16):
    level = block_scale(stream_key, extent, shards, -0.22, 0.18) if shards else 1.0
    drawn = jax.random.normal(stream_key, extent, jnp.float32) * spread * level
    return jnp.minimum(jnp.maximum(drawn, -most), most).astype(held_as)


def setup_inputs(seed: int = 0) -> dict:
    seeds = jax.random.split(jax.random.key(seed), 5)
    return {
        "query_rows": draw_query_rows(jax.random.fold_in(seeds[4], 71), 0),
        "key_rows": draw_key_rows(jax.random.fold_in(seeds[4], 71), 0),
        "value_rows": scatter_about(seeds[2], (TOKENS, HK * DH), 1.0, 6.0, ((0, 512),)),
        "selection": draw_selection(jax.random.fold_in(seeds[4], 71), 0),
    }


def block_terms(query_head, key_block, value_block, causal):
    length = key_block.shape[0]
    tile = min(512, query_head.shape[0])
    count = query_head.shape[0] // tile
    tiles = query_head.reshape(count, tile, query_head.shape[1])
    scale = query_head.shape[1] ** -0.5

    def one_tile(packed):
        rows_q, offset = packed
        scores = jnp.dot(rows_q, key_block.T, preferred_element_type=jnp.float32) * scale
        if causal:
            row_ids = offset + jnp.arange(tile, dtype=jnp.int32)[:, None]
            col_ids = jnp.arange(length, dtype=jnp.int32)[None, :]
            scores = jnp.where(col_ids <= row_ids, scores, -1e30)
        peak = jnp.max(scores, axis=1)
        expos = jnp.exp(scores - peak[:, None])
        mass = jnp.sum(expos, axis=1)
        summed = jnp.dot(expos.astype(jnp.bfloat16), value_block, preferred_element_type=jnp.float32)
        return peak, mass, summed

    peak, mass, summed = lax.map(one_tile, (tiles, jnp.arange(count, dtype=jnp.int32) * tile))
    return peak.reshape(-1), mass.reshape(-1), summed.reshape(-1, summed.shape[-1])


def reference(query_rows, key_rows, value_rows, selection):
    group = HQ // HK
    q_four = query_rows.reshape(NB, BLOCK, HQ, DH)
    k_four = key_rows.reshape(NB, BLOCK, HK, DH)
    v_four = value_rows.reshape(NB, BLOCK, HK, DH)

    def one_block(block_pos):
        chosen = selection[block_pos]
        q_block = lax.dynamic_index_in_dim(q_four, block_pos, 0, keepdims=False)

        def one_head(head_pos):
            kv_head = head_pos // group
            query_head = lax.dynamic_index_in_dim(q_block, head_pos, 1, keepdims=False)
            peaks = []
            masses = []
            sums = []
            for slot_pos in range(SLOTS):
                target = jnp.maximum(chosen[slot_pos], 0).astype(jnp.int32)
                key_block = lax.dynamic_index_in_dim(lax.dynamic_index_in_dim(k_four, target, 0, keepdims=False), kv_head, 1, keepdims=False)
                value_block = lax.dynamic_index_in_dim(lax.dynamic_index_in_dim(v_four, target, 0, keepdims=False), kv_head, 1, keepdims=False)
                peak, mass, summed = block_terms(query_head, key_block, value_block, slot_pos == 0)
                peaks.append(jnp.where(chosen[slot_pos] >= 0, peak, -1e30))
                masses.append(mass)
                sums.append(summed)
            top = jnp.maximum(jnp.maximum(peaks[0], peaks[1]), peaks[2])
            numer = jnp.zeros_like(sums[0])
            denom = jnp.zeros_like(masses[0])
            for slot_pos in range(SLOTS):
                factor = jnp.exp(peaks[slot_pos] - top)
                numer = numer + factor[:, None] * sums[slot_pos]
                denom = denom + factor * masses[slot_pos]
            return numer / denom[:, None]

        return lax.map(one_head, jnp.arange(HQ, dtype=jnp.int32))

    result = lax.map(one_block, jnp.arange(NB, dtype=jnp.int32))
    return result.transpose(0, 2, 1, 3).reshape(TOKENS, HQ * DH).astype(jnp.bfloat16)
```

```python
import functools

import jax
import jax.numpy as jnp
from jax import lax
from jax.experimental import pallas as pl
from jax.experimental.pallas import tpu as pltpu
from jax.sharding import PartitionSpec as P

DH = 128
BLOCK = 2048
SLOTS = 3
MESH = pl.DeviceIdType.MESH
LOG2E = 1.4426950408889634


def place():
    ctx = lax.axis_index("ctx")
    head = lax.axis_index("head")
    half, pair = ctx // 8, ctx % 8
    y, zlow = head // 8, head % 8
    return half, pair // 2, pair % 2, y, zlow


def device(half, pair, y, zlow):
    return (half * 8 + pair, y * 8 + zlow)


def spread_kernel(sel_ref, k_ref, v_ref, out_ref, ring, picked, landed,
                  a_send, a_recv, up_send, up_recv, down_send, down_recv, c_send, c_recv, o_sem):
    half, x, core, y, zlow = place()
    pair = x * 2 + core
    z = half * 8 + zlow
    above, below = (z + 1) % 16, (z + 15) % 16

    barrier = pltpu.get_barrier_semaphore()

    def hello(target):
        pl.semaphore_signal(barrier, inc=1, device_id=target, device_id_type=MESH)

    for src in range(8):
        @pl.when(jnp.logical_or(src != pair, x != y))
        def _():
            hello(device(half, src, x, zlow))
    hello(device(above // 8, pair, y, above % 8))
    hello(device(below // 8, pair, y, below % 8))
    for i in range(1, 8):
        hello(device(half, (pair + i) % 8, y, zlow))
    pl.semaphore_wait(barrier, jnp.where(x == y, 16, 17))

    def a_copy(kv, head, src, rows):
        return pltpu.make_async_remote_copy(
            src_ref=rows.at[:, pl.ds(head * DH, DH)],
            dst_ref=ring.at[z, src],
            send_sem=a_send.at[kv, head],
            recv_sem=a_recv.at[src],
            device_id=device(half, y * 2 + kv, head, zlow),
            device_id_type=MESH,
        )

    for kv, rows in ((0, k_ref), (1, v_ref)):
        for head in range(4):
            mine = jnp.logical_and(x == y, jnp.logical_and(core == kv, head == y))

            @pl.when(mine)
            def _():
                pltpu.make_async_copy(
                    rows.at[:, pl.ds(head * DH, DH)], ring.at[z, pair], a_recv.at[pair]
                ).start()

            @pl.when(jnp.logical_not(mine))
            def _():
                a_copy(kv, head, pair, rows).start()
    for src in range(8):
        pltpu.make_async_copy(ring.at[z, src], ring.at[z, src], a_recv.at[src]).wait()
    for kv, rows in ((0, k_ref), (1, v_ref)):
        for head in range(4):
            mine = jnp.logical_and(x == y, jnp.logical_and(core == kv, head == y))

            @pl.when(jnp.logical_not(mine))
            def _():
                a_copy(kv, head, pair, rows).wait_send()

    def r_copy(step, part, up):
        piece = (z + 16 - step) % 16 if up else (z + step) % 16
        to = above if up else below
        rows = ring.at[piece, pl.ds(part * 4, 4)]
        return pltpu.make_async_remote_copy(
            src_ref=rows,
            dst_ref=rows,
            send_sem=(up_send if up else down_send).at[step, part],
            recv_sem=(up_recv if up else down_recv).at[step, part],
            device_id=device(to // 8, pair, y, to % 8),
            device_id_type=MESH,
        )

    def r_wait(step, part, up):
        piece = (z + 16 - step - 1) % 16 if up else (z + step + 1) % 16
        rows = ring.at[piece, pl.ds(part * 4, 4)]
        pltpu.make_async_copy(rows, rows, (up_recv if up else down_recv).at[step, part]).wait()

    for step in range(8):
        for part in range(2):
            for up in (True, False):
                if not up and step == 7:
                    continue
                if step:
                    r_wait(step - 1, part, up)
                r_copy(step, part, up).start()
    for part in range(2):
        r_wait(7, part, True)
        r_wait(6, part, False)
    for step in range(8):
        for part in range(2):
            for up in (True, False):
                if not up and step == 7:
                    continue
                r_copy(step, part, up).wait_send()

    def c_copy(i, target, source):
        return pltpu.make_async_remote_copy(
            src_ref=picked.at[i - 1],
            dst_ref=landed.at[core, :, pl.ds(pl.multiple_of(x * 512, 512), 512)],
            send_sem=c_send.at[i - 1],
            recv_sem=c_recv.at[i - 1],
            device_id=device(half, target, y, zlow),
            device_id_type=MESH,
        )

    for i in (4, 3, 5, 2, 6, 1, 7, 0):
        target = (pair + i) % 8
        for slot in range(SLOTS):
            block = jnp.maximum(sel_ref[half * 8 + target, slot], 0)
            for piece in range(8):
                rows = ring[(block // 8) * 8 + piece, block % 8]
                if i:
                    picked[i - 1, slot, piece * 64:(piece + 1) * 64] = rows
                else:
                    landed[core, slot, pl.ds(pl.multiple_of(x * 512 + piece * 64, 64), 64)] = rows
        if i:
            c_copy(i, target, pair).start()
    for i in (4, 3, 5, 2, 6, 1, 7):
        source = (pair + 8 - i) % 8
        rows = landed.at[source % 2, :, pl.ds(pl.multiple_of(source // 2 * 512, 512), 512)]
        pltpu.make_async_copy(rows, rows, c_recv.at[i - 1]).wait()
        c_copy(i, (pair + i) % 8, pair).wait_send()
    copy = pltpu.make_async_copy(landed, out_ref, o_sem)
    copy.start()
    copy.wait()


def spread(key_rows, value_rows, selection):
    dma = pltpu.SemaphoreType.DMA
    return pl.pallas_call(
        spread_kernel,
        out_shape=jax.ShapeDtypeStruct((2, SLOTS, BLOCK, DH), jnp.bfloat16),
        in_specs=[
            pl.BlockSpec(memory_space=pltpu.SMEM),
            pl.BlockSpec(memory_space=pltpu.VMEM),
            pl.BlockSpec(memory_space=pltpu.VMEM),
        ],
        out_specs=pl.BlockSpec(memory_space=pl.ANY),
        scratch_shapes=[
            pltpu.VMEM((16, 8, 64, DH), jnp.bfloat16),
            pltpu.VMEM((7, SLOTS, 512, DH), jnp.bfloat16),
            pltpu.VMEM((2, SLOTS, BLOCK, DH), jnp.bfloat16),
            dma((2, 4)), dma((8,)),
            dma((8, 2)), dma((8, 2)), dma((8, 2)), dma((8, 2)),
            dma((7,)), dma((7,)), dma,
        ],
        compiler_params=pltpu.CompilerParams(
            collective_id=0, has_side_effects=True, vmem_limit_bytes=48 * 2**20
        ),
        name="spread_blocks",
    )(selection, key_rows, value_rows)


def attend_kernel(bq, bk, sel_ref, q_ref, kv_ref, out_ref, acc):
    ctx = lax.axis_index("ctx")
    tile = pl.program_id(0)
    factor = DH**-0.5 * LOG2E
    q = q_ref[...]

    acc[...] = jnp.zeros_like(acc)
    peak0 = jnp.full((bq, 128), -1e30, jnp.float32)

    def block_step(slot, chunk, peak, causal):
        start = pl.multiple_of(chunk * bk, bk)
        keys = kv_ref[0, slot, pl.ds(start, bk)]
        values = kv_ref[1, slot, pl.ds(start, bk)]
        scores = lax.dot_general(
            q, keys, (((1,), (1,)), ((), ())), preferred_element_type=jnp.float32
        )
        if causal:
            rows = lax.broadcasted_iota(jnp.int32, scores.shape, 0) + tile * bq
            cols = lax.broadcasted_iota(jnp.int32, scores.shape, 1) + start
            scores = jnp.where(cols <= rows, scores, -1e30)
        top = jnp.maximum(peak, jnp.max(scores, axis=1, keepdims=True))
        weights = jnp.exp2(scores * factor - (top * factor)[:, :1]).astype(jnp.bfloat16)
        widened = jnp.concatenate([values, jnp.ones_like(values)], axis=1)
        before = jnp.exp2((peak - top) * factor)[:, :1]
        acc[...] = acc[...] * before + jnp.dot(
            weights, widened, preferred_element_type=jnp.float32
        )
        return top

    def full(i, peak):
        return block_step(0, i, peak, False)

    peak = lax.fori_loop(0, tile * bq // bk, full, peak0)
    peak = block_step(0, tile * bq // bk, peak, True)
    for slot in range(1, SLOTS):
        live = sel_ref[ctx, slot] >= 0

        def more(i, peak):
            return block_step(slot, i, peak, False)

        peak = lax.fori_loop(0, jnp.where(live, BLOCK // bk, 0), more, peak)
    out_ref[...] = (acc[:, :DH] / acc[:, DH:]).astype(out_ref.dtype)


def attend(query_rows, kv, selection, bq=512, bk=512):
    return pl.pallas_call(
        functools.partial(attend_kernel, bq, bk),
        out_shape=jax.ShapeDtypeStruct(query_rows.shape, jnp.bfloat16),
        grid=(BLOCK // bq,),
        in_specs=[
            pl.BlockSpec(memory_space=pltpu.SMEM),
            pl.BlockSpec((bq, DH), lambda i: (i, 0)),
            pl.BlockSpec((2, SLOTS, BLOCK, DH), lambda i: (0, 0, 0, 0)),
        ],
        out_specs=pl.BlockSpec((bq, DH), lambda i: (i, 0)),
        scratch_shapes=[pltpu.VMEM((bq, 2 * DH), jnp.float32)],
        compiler_params=pltpu.CompilerParams(vmem_limit_bytes=40 * 2**20),
        name="attend_blocks",
    )(selection, query_rows, kv)


def on_device(query_rows, key_rows, value_rows, selection):
    kv = spread(key_rows, value_rows, selection)
    return attend(query_rows, kv, selection)


def solution(mesh):
    placed = (P("ctx", "head"), P(("ctx", "head"), None), P(("ctx", "head"), None), P())
    return jax.shard_map(
        on_device, mesh=mesh, in_specs=placed, out_specs=P("ctx", "head"), check_vma=False
    )
```

```python
import functools

import jax
import jax.numpy as jnp
from jax import lax
from jax.experimental import pallas as pl
from jax.experimental.pallas import tpu as pltpu
from jax.sharding import PartitionSpec as P

DH = 128
BLOCK = 2048
SLOTS = 3
PARTS = 4
TILE = 256
MESH = pl.DeviceIdType.MESH
FACTOR = DH**-0.5 * 1.4426950408889634
ROUNDS = (
    ("U4", "D4"), ("D3", "U5"), ("U3", "D5"), ("D2", "U6"),
    ("U2", "D6"), ("D1", "U7"), ("U1", "D7"), ("U0", "U8"),
)


def place():
    ctx = lax.axis_index("ctx")
    head = lax.axis_index("head")
    half, pair = ctx // 8, ctx % 8
    y, zlow = head // 8, head % 8
    return half, pair // 2, pair % 2, y, zlow


def device(half, pair, y, zlow):
    return (half * 8 + pair, y * 8 + zlow)


def fused_kernel(sel_hbm, q_hbm, k_hbm, v_hbm, out_ref, *scratch):
    ups, downs = scratch[:9], scratch[9:16]
    (sel_ref, q_ref, picked, land0, land, nat, peak, acc, l_sem,
     a_send, a_recv, up_send, up_recv, down_send, down_recv,
     o_send, o_recv, c_send, c_recv) = scratch[16:]
    half, x, core, y, zlow = place()
    ctx = lax.axis_index("ctx")
    pair = x * 2 + core
    z = half * 8 + zlow
    above, below = (z + 1) % 16, (z + 15) % 16

    def buffer(name):
        return ups[int(name[1])] if name[0] == "U" else downs[int(name[1]) - 1]

    def half_of(name):
        s = int(name[1])
        return ((z + 16 - s) % 16 if name[0] == "U" else (z + s) % 16) // 8

    load_sel = pltpu.make_async_copy(sel_hbm, sel_ref, l_sem.at[0])
    load_sel.start()
    load_q = pltpu.make_async_copy(q_hbm, q_ref, l_sem.at[1])
    load_q.start()

    barrier = pltpu.get_barrier_semaphore()

    def hello(target):
        pl.semaphore_signal(barrier, inc=1, device_id=target, device_id_type=MESH)

    for src in range(8):
        for part in range(2):
            origin = (x + 8 - src // 2 - 2 * part) % 4

            @pl.when(jnp.logical_or(src != pair, origin != y))
            def _():
                hello(device(half, src, origin, zlow))
    hello(device(above // 8, pair, y, above % 8))
    hello(device(below // 8, pair, y, below % 8))
    for i in range(1, 8):
        hello(device(half, (pair + i) % 8, y, zlow))
    pl.semaphore_wait(barrier, jnp.where(y % 2 == 0, 24, 25))

    def a_copies():
        for kv, rows in ((0, k_hbm), (1, v_hbm)):
            for head in range(4):
                for part in range(2):
                    mine = jnp.logical_and(
                        (y + 2 * part) % 4 == 0, jnp.logical_and(core == kv, head == y)
                    )
                    src = rows.at[pl.ds(part * 32, 32), pl.ds(head * DH, DH)]
                    dst = ups[0].at[pair, pl.ds(part * 32, 32)]
                    yield mine, pltpu.make_async_copy(src, dst, a_recv.at[pair, part]), (
                        pltpu.make_async_remote_copy(
                            src_ref=src,
                            dst_ref=dst,
                            send_sem=a_send.at[kv, head, part],
                            recv_sem=a_recv.at[pair, part],
                            device_id=device(half, (x + y + 2 * part) % 4 * 2 + kv, head, zlow),
                            device_id_type=MESH,
                        )
                    )

    for mine, local, remote in a_copies():
        pl.when(mine)(local.start)
        pl.when(jnp.logical_not(mine))(remote.start)
    for src in range(8):
        for part in range(2):
            rows = ups[0].at[src, pl.ds(part * 32, 32)]
            pltpu.make_async_copy(rows, rows, a_recv.at[src, part]).wait()
    load_sel.wait()

    width = 8 // PARTS

    def ring_copy(step, part, up):
        bufs = ups if up else (ups[0],) + tuple(downs)
        to = above if up else below
        return pltpu.make_async_remote_copy(
            src_ref=bufs[step].at[pl.ds(part * width, width)],
            dst_ref=bufs[step + 1].at[pl.ds(part * width, width)],
            send_sem=(up_send if up else down_send).at[step, part],
            recv_sem=(up_recv if up else down_recv).at[step, part],
            device_id=device(to // 8, pair, y, to % 8),
            device_id_type=MESH,
        )

    def own_sends(name, zpos):
        buf = buffer(name)
        rows = pl.ds(pl.multiple_of(zpos * 64, 64), 64)
        for i in (4, 3, 5, 2, 6, 1, 7):
            target = (pair + i) % 8
            pltpu.make_async_remote_copy(
                src_ref=buf.at[target],
                dst_ref=land0.at[core, x, rows],
                send_sem=o_send.at[i - 1],
                recv_sem=o_recv.at[i - 1],
                device_id=device(half, target, y, zlow),
                device_id_type=MESH,
            ).start()
        land0[core, x, rows] = buf[pair]

    def picked_copy(i, t):
        return pltpu.make_async_remote_copy(
            src_ref=picked.at[i - 1, t],
            dst_ref=land.at[core, t, :, x],
            send_sem=c_send.at[i - 1, t],
            recv_sem=c_recv.at[i - 1, t],
            device_id=device(half, (pair + i) % 8, y, zlow),
            device_id_type=MESH,
        )

    def picked_sends(t):
        one, two = ROUNDS[t]
        for i in (4, 3, 5, 2, 6, 1, 7, 0):
            target = (pair + i) % 8
            for slot in range(2):
                block = jnp.maximum(sel_ref[slot + 1, half * 8 + target], 0)
                rows = jnp.where(
                    block // 8 == half_of(one), buffer(one)[block % 8], buffer(two)[block % 8]
                )
                if i:
                    picked[i - 1, t, slot] = rows
                else:
                    land[core, t, slot, x] = rows
            if i:
                picked_copy(i, t).start()

    for step in range(9):
        for part in range(PARTS):
            for up in (True, False):
                last = 8 if up else 7
                if 0 < step <= last:
                    ring_copy(step - 1, part, up).wait_recv()
                if step < last:
                    ring_copy(step, part, up).start()
        if step == 0:
            own_sends("U0", zlow)
        elif step < 8:
            pl.when(zlow >= step)(functools.partial(own_sends, "U%d" % step, zlow - step))
            pl.when(zlow + step < 8)(functools.partial(own_sends, "D%d" % step, zlow + step))
        for t in range(8):
            if step == 4 + (t + 1) // 2:
                picked_sends(t)

    load_q.wait()
    for i in range(1, 8):
        src = (pair + 8 - i) % 8
        rows = land0.at[src % 2, src // 2]
        pltpu.make_async_copy(rows, rows, o_recv.at[i - 1]).wait()
    for src in range(4):
        for part in range(2):
            origin = (src + 8 - x - 2 * part) % 4

            def settle(zpos, _):
                start = pl.multiple_of(zpos * 64 + part * 32, 32)
                there = pl.multiple_of(origin * 512 + zpos * 64 + part * 32, 32)
                for kv in range(2):
                    nat[kv, pl.ds(there, 32)] = land0[kv, src, pl.ds(start, 32)]
                return 0

            lax.fori_loop(0, 8, settle, 0)

    def scores_of(q, keys):
        return lax.dot_general(
            q, keys, (((1,), (1,)), ((), ())), preferred_element_type=jnp.float32
        )

    def widened(values):
        return jnp.concatenate([values, jnp.ones_like(values)], axis=1)

    if True:
        for tile in range(BLOCK // TILE):
            rows = pl.ds(tile * TILE, TILE)
            count = (tile + 1) * TILE
            scores = scores_of(q_ref[rows], nat[0, :count])
            row_ids = lax.broadcasted_iota(jnp.int32, (TILE, TILE), 0)
            col_ids = lax.broadcasted_iota(jnp.int32, (TILE, TILE), 1)
            edge = jnp.where(col_ids <= row_ids, scores[:, count - TILE:], -1e30)
            scores = jnp.concatenate([scores[:, :count - TILE], edge], axis=1) if tile else edge
            top = jnp.max(scores, axis=1, keepdims=True)
            weights = jnp.exp2((scores - top) * FACTOR).astype(jnp.bfloat16)
            peak[rows] = jnp.broadcast_to(top, (TILE, DH))
            acc[rows] = jnp.dot(weights, widened(nat[1, :count]), preferred_element_type=jnp.float32)

    def absorb(t, masked):
        keys = land[0, t].reshape(512, DH)
        values = widened(land[1, t].reshape(512, DH))
        for tile in range(BLOCK // TILE):
            rows = pl.ds(tile * TILE, TILE)
            scores = scores_of(q_ref[rows], keys)
            if masked:
                cols = lax.broadcasted_iota(jnp.int32, scores.shape, 1)
                chosen = jnp.where(cols < 256, sel_ref[1, ctx], sel_ref[2, ctx])
                scores = jnp.where(chosen >= 0, scores, -1e30)
            old = peak[rows]
            top = jnp.maximum(old, jnp.max(scores, axis=1, keepdims=True))
            weights = jnp.exp2((scores - top[:, :1]) * FACTOR).astype(jnp.bfloat16)
            before = jnp.exp2((old - top) * FACTOR)
            peak[rows] = top
            acc[rows] = acc[rows] * jnp.concatenate([before, before], axis=1) + jnp.dot(
                weights, values, preferred_element_type=jnp.float32
            )

    def round_of(t, _):
        for i in range(1, 8):
            src = (pair + 8 - i) % 8
            rows = land.at[src % 2, t, :, src // 2]
            pltpu.make_async_copy(rows, rows, c_recv.at[i - 1, t]).wait()
        pl.when(ctx < 2)(lambda: absorb(t, True))
        pl.when(ctx >= 2)(lambda: absorb(t, False))
        return 0

    lax.fori_loop(0, 8, round_of, 0)
    for tile in range(BLOCK // TILE):
        rows = pl.ds(tile * TILE, TILE)
        out_ref[rows] = (acc[rows, :DH] / acc[rows, DH:]).astype(out_ref.dtype)

    for mine, local, remote in a_copies():
        pl.when(jnp.logical_not(mine))(remote.wait_send)
    for step in range(8):
        for part in range(PARTS):
            ring_copy(step, part, True).wait_send()
            if step < 7:
                ring_copy(step, part, False).wait_send()
    for i in range(1, 8):
        pltpu.make_async_copy(land0.at[0, 0], land0.at[0, 0], o_send.at[i - 1]).wait()
        for t in range(8):
            picked_copy(i, t).wait_send()


def fused(query_rows, key_rows, value_rows, selection):
    dma = pltpu.SemaphoreType.DMA
    anywhere = pl.BlockSpec(memory_space=pl.ANY)
    bf16 = jnp.bfloat16
    return pl.pallas_call(
        fused_kernel,
        out_shape=jax.ShapeDtypeStruct((BLOCK, DH), bf16),
        in_specs=[anywhere] * 4,
        out_specs=pl.BlockSpec(memory_space=pltpu.VMEM),
        scratch_shapes=[pltpu.VMEM((8, 64, DH), bf16)] * 16 + [
            pltpu.SMEM((SLOTS, 16), jnp.int32),
            pltpu.VMEM((BLOCK, DH), bf16),
            pltpu.VMEM((7, 8, 2, 64, DH), bf16),
            pltpu.VMEM((2, 4, 512, DH), bf16),
            pltpu.VMEM((2, 8, 2, 4, 64, DH), bf16),
            pltpu.VMEM((2, BLOCK, DH), bf16),
            pltpu.VMEM((BLOCK, DH), jnp.float32),
            pltpu.VMEM((BLOCK, 2 * DH), jnp.float32),
            dma((2,)),
            dma((2, 4, 2)), dma((8, 2)),
            dma((8, PARTS)), dma((8, PARTS)), dma((8, PARTS)), dma((8, PARTS)),
            dma((7,)), dma((7,)), dma((7, 8)), dma((7, 8)),
        ],
        compiler_params=pltpu.CompilerParams(
            collective_id=0, has_side_effects=True, vmem_limit_bytes=60 * 2**20
        ),
        name="block_attention",
    )(selection.T, query_rows, key_rows, value_rows)


def solution(mesh):
    placed = (P("ctx", "head"), P(("ctx", "head"), None), P(("ctx", "head"), None), P())
    return jax.shard_map(
        fused, mesh=mesh, in_specs=placed, out_specs=P("ctx", "head"), check_vma=False
    )
```

```python
import jax
import jax.numpy as jnp
from jax import lax
from jax.experimental import pallas as pl
from jax.experimental.pallas import tpu as pltpu
from jax.sharding import PartitionSpec as P

DH = 128
BLOCK = 2048
SLOTS = 3
PARTS = 4
TILE = 256
MESH = pl.DeviceIdType.MESH
FACTOR = DH**-0.5 * 1.4426950408889634
ROUNDS = (
    ("U4", "D4"), ("D3", "U5"), ("U3", "D5"), ("D2", "U6"),
    ("U2", "D6"), ("D1", "U7"), ("U1", "D7"), ("U0", "U8"),
)


def place():
    ctx = lax.axis_index("ctx")
    head = lax.axis_index("head")
    half, pair = ctx // 8, ctx % 8
    y, zlow = head // 8, head % 8
    return half, pair // 2, pair % 2, y, zlow


def device(half, pair, y, zlow):
    return (half * 8 + pair, y * 8 + zlow)


def fused_kernel(sel_hbm, q_hbm, k_hbm, v_hbm, out_ref, *scratch):
    ups, downs = scratch[:9], scratch[9:16]
    (sel_ref, q_ref, picked, land0, land, nat, peak, acc, l_sem,
     a_send, a_recv, up_send, up_recv, down_send, down_recv,
     o_send, o_recv, c_send, c_recv) = scratch[16:]
    half, x, core, y, zlow = place()
    ctx = lax.axis_index("ctx")
    pair = x * 2 + core
    z = half * 8 + zlow
    above, below = (z + 1) % 16, (z + 15) % 16
    early, late = half == 0, half == 1

    def buffer(name):
        return ups[int(name[1])] if name[0] == "U" else downs[int(name[1]) - 1]

    def half_of(name):
        s = int(name[1])
        return ((z + 16 - s) % 16 if name[0] == "U" else (z + s) % 16) // 8

    def in_line(name):
        s = int(name[1])
        return zlow >= s if name[0] == "U" else zlow + s < 8

    load_sel = pltpu.make_async_copy(sel_hbm, sel_ref, l_sem.at[0])
    load_sel.start()

    barrier = pltpu.get_barrier_semaphore()

    def hello(target):
        pl.semaphore_signal(barrier, inc=1, device_id=target, device_id_type=MESH)

    for src in range(8):
        for part in range(2):
            origin = (x + 8 - src // 2 - 2 * part) % 4

            @pl.when(jnp.logical_or(src != pair, origin != y))
            def _():
                hello(device(half, src, origin, zlow))
    hello(device(above // 8, pair, y, above % 8))
    hello(device(below // 8, pair, y, below % 8))
    for i in range(1, 8):
        hello(device(half, (pair + i) % 8, y, zlow))
    pl.semaphore_wait(barrier, jnp.where(y % 2 == 0, 24, 25))

    def first(act):
        for head in range(4):
            for part in range(2):
                for kv, rows in ((0, k_hbm), (1, v_hbm)):
                    mine = jnp.logical_and(
                        (y + 2 * part) % 4 == 0, jnp.logical_and(core == kv, head == y)
                    )
                    src = rows.at[pl.ds(part * 32, 32), pl.ds(head * DH, DH)]
                    dst = ups[0].at[pair, pl.ds(part * 32, 32)]

                    @pl.when(jnp.logical_not(mine))
                    def _():
                        copy = pltpu.make_async_remote_copy(
                            src_ref=src,
                            dst_ref=dst,
                            send_sem=a_send.at[kv, head, part],
                            recv_sem=a_recv.at[pair, part],
                            device_id=device(half, (x + y + 2 * part) % 4 * 2 + kv, head, zlow),
                            device_id_type=MESH,
                        )
                        copy.start() if act else copy.wait_send()

                    if act:
                        @pl.when(mine)
                        def _():
                            pltpu.make_async_copy(src, dst, a_recv.at[pair, part]).start()

    first(True)
    load_q = pltpu.make_async_copy(q_hbm, q_ref, l_sem.at[1])
    load_q.start()

    width = 8 // PARTS

    def ring_copy(step, part, up):
        bufs = ups if up else (ups[0],) + tuple(downs)
        to = above if up else below
        return pltpu.make_async_remote_copy(
            src_ref=bufs[step].at[pl.ds(part * width, width)],
            dst_ref=bufs[step + 1].at[pl.ds(part * width, width)],
            send_sem=(up_send if up else down_send).at[step, part],
            recv_sem=(up_recv if up else down_recv).at[step, part],
            device_id=device(to // 8, pair, y, to % 8),
            device_id_type=MESH,
        )

    def held(step, up):
        return jnp.logical_or(late, in_line(("U" if up else "D") + str(step)))

    def passed_on(step, up):
        edge = zlow == (7 if up else 0)
        return jnp.logical_and(held(step, up), jnp.logical_not(jnp.logical_and(late, edge)))

    def own_sends(name):
        buf = buffer(name)
        s = int(name[1])
        zpos = zlow - s if name[0] == "U" else zlow + s
        rows = pl.ds(pl.multiple_of(zpos * 64, 64), 64)
        for i in (4, 3, 5, 2, 6, 1, 7):
            target = (pair + i) % 8
            pltpu.make_async_remote_copy(
                src_ref=buf.at[target],
                dst_ref=land0.at[core, x, rows],
                send_sem=o_send.at[i - 1],
                recv_sem=o_recv.at[i - 1],
                device_id=device(half, target, y, zlow),
                device_id_type=MESH,
            ).start()
        land0[core, x, rows] = buf[pair]

    def picked_copy(i, t):
        return pltpu.make_async_remote_copy(
            src_ref=picked.at[i, t],
            dst_ref=land.at[core, t, :, x],
            send_sem=c_send.at[i, t],
            recv_sem=c_recv.at[i, t],
            device_id=device(half, (pair + i) % 8, y, zlow),
            device_id_type=MESH,
        )

    def block_for(row, slot):
        block = sel_ref[slot + 1, row]
        return jnp.maximum(jnp.where(block < 0, sel_ref[2 - slot, row], block), 0)

    def picked_sends(t, one, two=None):
        def rows_for(row, slot):
            block = block_for(row, slot)
            rows = buffer(one)[block % 8]
            if two is not None:
                rows = jnp.where(block // 8 == half_of(one), rows, buffer(two)[block % 8])
            return rows

        def to(n, _):
            i = (3 + n) % 7 + 1
            for slot in range(2):
                picked[i, t, slot] = rows_for(half * 8 + (pair + i) % 8, slot)
            picked_copy(i, t).start()
            return 0

        lax.fori_loop(0, 7, to, 0)
        for slot in range(2):
            land[core, t, slot, x] = rows_for(ctx, slot)

    turn = {}
    for t, names in enumerate(ROUNDS):
        for name in names:
            turn[name] = t

    for step in range(9):
        for part in range(PARTS):
            if step == 0:
                for src in range(part * width, (part + 1) * width):
                    for cut in range(2):
                        rows = ups[0].at[src, pl.ds(cut * 32, 32)]
                        pltpu.make_async_copy(rows, rows, a_recv.at[src, cut]).wait()
            for up in (True, False):
                last = 8 if up else 7
                if 0 < step <= last:
                    pl.when(held(step, up))(lambda: ring_copy(step - 1, part, up).wait_recv())
                if step < last:
                    pl.when(passed_on(step, up))(lambda: ring_copy(step, part, up).start())
        names = lambda s: ["U0"] if s == 0 else ["U%d" % s, "D%d" % s]
        if step == 0:
            load_sel.wait()
        if step < 8:
            for name in names(step):
                pl.when(in_line(name))(lambda: own_sends(name))
        if step > 0:
            for name in names(step - 1):
                pl.when(jnp.logical_and(early, in_line(name)))(
                    lambda: picked_sends(turn[name], name)
                )
        for t in range(8):
            if step == 4 + (t + 1) // 2:
                pl.when(late)(lambda: picked_sends(t, *ROUNDS[t]))

    load_q.wait()

    def scores_of(q, keys):
        return lax.dot_general(
            q, keys, (((1,), (1,)), ((), ())), preferred_element_type=jnp.float32
        )

    peak[...] = jnp.full_like(peak, -1e30)
    acc[...] = jnp.zeros_like(acc)

    def absorb(rows, scores, values):
        old = peak[rows]
        top = jnp.maximum(old, jnp.max(scores, axis=1, keepdims=True))
        weights = jnp.exp2((scores - top[:, :1]) * FACTOR).astype(jnp.bfloat16)
        before = jnp.exp2((old - top) * FACTOR)
        peak[rows] = top
        acc[rows] = acc[rows] * jnp.concatenate([before, before], axis=1) + jnp.dot(
            weights, values, preferred_element_type=jnp.float32
        )

    def own_block():
        for i in range(1, 8):
            src = (pair + 8 - i) % 8
            rows = land0.at[src % 2, src // 2]
            pltpu.make_async_copy(rows, rows, o_recv.at[i - 1]).wait()
        for src in range(4):
            for part in range(2):
                origin = (src + 8 - x - 2 * part) % 4

                def settle(zpos, _):
                    start = pl.multiple_of(zpos * 64 + part * 32, 32)
                    there = pl.multiple_of(origin * 512 + zpos * 64 + part * 32, 32)
                    for kv in range(2):
                        nat[kv, pl.ds(there, 32)] = land0[kv, src, pl.ds(start, 32)]
                    return 0

                lax.fori_loop(0, 8, settle, 0)
        for tile in range(BLOCK // TILE):
            rows = pl.ds(tile * TILE, TILE)
            count = (tile + 1) * TILE
            scores = scores_of(q_ref[rows], nat[0, :count])
            row_ids = lax.broadcasted_iota(jnp.int32, (TILE, TILE), 0)
            col_ids = lax.broadcasted_iota(jnp.int32, (TILE, TILE), 1)
            edge = jnp.where(col_ids <= row_ids, scores[:, count - TILE:], -1e30)
            scores = jnp.concatenate([scores[:, :count - TILE], edge], axis=1) if tile else edge
            values = nat[1, :count]
            absorb(rows, scores, jnp.concatenate([values, jnp.ones_like(values)], axis=1))

    def round_at(k):
        step = jnp.where(k % 2 == 1, -((k + 1) // 2), k // 2)
        near = jnp.minimum(zlow, 7 - zlow)
        far = jnp.where(zlow < 4, k - zlow, 7 - k - zlow)
        away = (jnp.where(k <= 2 * near, step, far) + 8) % 8
        return jnp.where(late, k, jnp.where(away <= 4, jnp.maximum(7 - 2 * away, 0), 2 * away - 8))

    def group(g):
        turns = [round_at(2 * g), round_at(2 * g + 1)]
        for t in turns:
            for i in range(1, 8):
                src = (pair + 8 - i) % 8
                rows = land.at[src % 2, t, :, src // 2]
                pltpu.make_async_copy(rows, rows, c_recv.at[i, t]).wait()

        @pl.when(ctx > 0)
        def _():
            slots = lax.broadcasted_iota(jnp.int32, (2, 256, DH), 0).reshape(512, DH)
            live = jnp.where(slots == 0, sel_ref[1, ctx], sel_ref[2, ctx]) >= 0
            ones = jnp.where(live, 1.0, 0.0).astype(jnp.bfloat16)
            keys = jnp.concatenate([land[0, t].reshape(512, DH) for t in turns], axis=0)
            values = jnp.concatenate(
                [
                    jnp.concatenate([land[1, t].reshape(512, DH) * ones, ones], axis=1)
                    for t in turns
                ],
                axis=0,
            )
            for tile in range(BLOCK // TILE):
                rows = pl.ds(tile * TILE, TILE)
                absorb(rows, scores_of(q_ref[rows], keys), values)

    own_turn = jnp.where(late, jnp.maximum(zlow, 7 - zlow) - 4, 3)

    def work(g, _):
        pl.when(g == own_turn)(own_block)
        group(g)
        return 0

    lax.fori_loop(0, 4, work, 0)
    for tile in range(BLOCK // TILE):
        rows = pl.ds(tile * TILE, TILE)
        out_ref[rows] = (acc[rows, :DH] / acc[rows, DH:]).astype(out_ref.dtype)

    first(False)
    for step in range(8):
        for up in (True, False):
            if up or step < 7:
                @pl.when(passed_on(step, up))
                def _():
                    for part in range(PARTS):
                        ring_copy(step, part, up).wait_send()
    for i in range(1, 8):
        pltpu.make_async_copy(land0.at[0, 0], land0.at[0, 0], o_send.at[i - 1]).wait()
        for t in range(8):
            picked_copy(i, t).wait_send()


def fused(query_rows, key_rows, value_rows, selection):
    dma = pltpu.SemaphoreType.DMA
    anywhere = pl.BlockSpec(memory_space=pl.ANY)
    bf16 = jnp.bfloat16
    return pl.pallas_call(
        fused_kernel,
        out_shape=jax.ShapeDtypeStruct((BLOCK, DH), bf16),
        in_specs=[anywhere] * 4,
        out_specs=pl.BlockSpec(memory_space=pltpu.VMEM),
        scratch_shapes=[pltpu.VMEM((8, 64, DH), bf16)] * 16 + [
            pltpu.SMEM((SLOTS, 16), jnp.int32),
            pltpu.VMEM((BLOCK, DH), bf16),
            pltpu.VMEM((8, 8, 2, 64, DH), bf16),
            pltpu.VMEM((2, 4, 512, DH), bf16),
            pltpu.VMEM((2, 8, 2, 4, 64, DH), bf16),
            pltpu.VMEM((2, BLOCK, DH), bf16),
            pltpu.VMEM((BLOCK, DH), jnp.float32),
            pltpu.VMEM((BLOCK, 2 * DH), jnp.float32),
            dma((2,)),
            dma((2, 4, 2)), dma((8, 2)),
            dma((8, PARTS)), dma((8, PARTS)), dma((8, PARTS)), dma((8, PARTS)),
            dma((7,)), dma((7,)), dma((8, 8)), dma((8, 8)),
        ],
        compiler_params=pltpu.CompilerParams(
            collective_id=0, has_side_effects=True, vmem_limit_bytes=60 * 2**20
        ),
        name="block_attention",
    )(selection.T, query_rows, key_rows, value_rows)


def solution(mesh):
    placed = (P("ctx", "head"), P(("ctx", "head"), None), P(("ctx", "head"), None), P())
    return jax.shard_map(
        fused, mesh=mesh, in_specs=placed, out_specs=P("ctx", "head"), check_vma=False
    )
```

```python
import functools

import jax
import jax.numpy as jnp
from jax import lax
from jax.experimental import pallas as pl
from jax.experimental.pallas import tpu as pltpu
from jax.sharding import PartitionSpec as P

DH = 128
BLOCK = 2048
SLOTS = 3
PARTS = 4
TILE = 256
MESH = pl.DeviceIdType.MESH
FACTOR = DH**-0.5 * 1.4426950408889634
LEAST, MOST = 2.0**-80, 2.0**100


def place():
    ctx = lax.axis_index("ctx")
    head = lax.axis_index("head")
    half, pair = ctx // 8, ctx % 8
    y, zlow = head // 8, head % 8
    return half, pair // 2, pair % 2, y, zlow


def device(half, pair, y, zlow):
    return (half * 8 + pair, y * 8 + zlow)


def fused_kernel(sel_hbm, q_hbm, k_hbm, v_hbm, out_ref, bad_ref, own_hbm, kv_hbm, *scratch):
    ups, downs = scratch[:9], scratch[9:16]
    (sel_ref, q_ref, picked, land0, land, nat, acc, l_sem, w_sem,
     a_send, a_recv, up_send, up_recv, down_send, down_recv,
     o_send, o_recv, c_send, c_recv, ready) = scratch[16:]
    half, x, core, y, zlow = place()
    ctx = lax.axis_index("ctx")
    pair = x * 2 + core
    z = half * 8 + zlow
    above, below = (z + 1) % 16, (z + 15) % 16
    early, late = half == 0, half == 1

    def buffer(name):
        return ups[int(name[1])] if name[0] == "U" else downs[int(name[1]) - 1]

    def in_line(name):
        s = int(name[1])
        return zlow >= s if name[0] == "U" else zlow + s < 8

    load_sel = pltpu.make_async_copy(sel_hbm, sel_ref, l_sem.at[0])
    load_sel.start()

    barrier = pltpu.get_barrier_semaphore()

    def hello(target):
        pl.semaphore_signal(barrier, inc=1, device_id=target, device_id_type=MESH)

    for src in range(8):
        for part in range(2):
            origin = (x + 8 - src // 2 - 2 * part) % 4

            @pl.when(jnp.logical_or(src != pair, origin != y))
            def _():
                hello(device(half, src, origin, zlow))
    pl.when(z < 15)(lambda: hello(device(above // 8, pair, y, above % 8)))
    hello(device(below // 8, pair, y, below % 8))
    for i in range(1, 8):
        hello(device(half, (pair + i) % 8, y, zlow))
    pl.semaphore_wait(barrier, 25 - jnp.where(y % 2 == 0, 1, 0) - jnp.where(z == 0, 1, 0))

    @pl.when(z == 15)
    def _():
        pl.semaphore_signal(ready, inc=1, device_id=device(0, pair, y, 0), device_id_type=MESH)

    def first(act):
        for head in range(4):
            for part in range(2):
                for kv, rows in ((0, k_hbm), (1, v_hbm)):
                    mine = jnp.logical_and(
                        (y + 2 * part) % 4 == 0, jnp.logical_and(core == kv, head == y)
                    )
                    src = rows.at[pl.ds(part * 32, 32), pl.ds(head * DH, DH)]
                    dst = ups[0].at[pair, pl.ds(part * 32, 32)]

                    @pl.when(jnp.logical_not(mine))
                    def _():
                        copy = pltpu.make_async_remote_copy(
                            src_ref=src,
                            dst_ref=dst,
                            send_sem=a_send.at[kv, head, part],
                            recv_sem=a_recv.at[pair, part],
                            device_id=device(half, (x + y + 2 * part) % 4 * 2 + kv, head, zlow),
                            device_id_type=MESH,
                        )
                        copy.start() if act else copy.wait_send()

                    if act:
                        @pl.when(mine)
                        def _():
                            pltpu.make_async_copy(src, dst, a_recv.at[pair, part]).start()

    first(True)
    load_q = pltpu.make_async_copy(q_hbm, q_ref, l_sem.at[1])
    load_q.start()

    width = 8 // PARTS

    def ring_copy(step, part, up):
        bufs = ups if up else (ups[0],) + tuple(downs)
        to = above if up else below
        return pltpu.make_async_remote_copy(
            src_ref=bufs[step].at[pl.ds(part * width, width)],
            dst_ref=bufs[step + 1].at[pl.ds(part * width, width)],
            send_sem=(up_send if up else down_send).at[step, part],
            recv_sem=(up_recv if up else down_recv).at[step, part],
            device_id=device(to // 8, pair, y, to % 8),
            device_id_type=MESH,
        )

    def held(step, up):
        return jnp.logical_or(late, in_line(("U" if up else "D") + str(step)))

    def passed_on(step, up):
        edge = zlow == (7 if up else 0)
        return jnp.logical_and(held(step, up), jnp.logical_not(jnp.logical_and(late, edge)))

    def own_sends(name):
        buf = buffer(name)
        s = int(name[1])
        zpos = zlow - s if name[0] == "U" else zlow + s
        rows = pl.ds(pl.multiple_of(zpos * 64, 64), 64)
        for i in (4, 3, 5, 2, 6, 1, 7):
            target = (pair + i) % 8
            pltpu.make_async_remote_copy(
                src_ref=buf.at[target],
                dst_ref=land0.at[core, x, rows],
                send_sem=o_send.at[i - 1],
                recv_sem=o_recv.at[i - 1],
                device_id=device(half, target, y, zlow),
                device_id_type=MESH,
            ).start()
        land0[core, x, rows] = buf[pair]

    def picked_copy(i, t):
        return pltpu.make_async_remote_copy(
            src_ref=picked.at[i, t],
            dst_ref=land.at[core, t, :, x],
            send_sem=c_send.at[i, t],
            recv_sem=c_recv.at[i, t],
            device_id=device(half, (pair + i) % 8, y, zlow),
            device_id_type=MESH,
        )

    def block_for(row, slot):
        block = sel_ref[slot + 1, row]
        return jnp.maximum(jnp.where(block < 0, sel_ref[2 - slot, row], block), 0)

    def picks(name, t, merge):
        def to(n, _):
            i = (n + 4) % 8
            for slot in range(2):
                block = block_for(half * 8 + (pair + i) % 8, slot)
                rows = buffer(name)[block % 8]
                if merge:
                    rows = jnp.where(block < 8, rows, picked[i, t, slot])
                picked[i, t, slot] = rows
            if merge:
                pl.when(i > 0)(lambda: picked_copy(i, t).start())
            else:
                pl.when(jnp.logical_and(early, i > 0))(lambda: picked_copy(i, t).start())
            return 0

        lax.fori_loop(0, 8, to, 0)

        def keep():
            for slot in range(2):
                land[core, t, slot, x] = picked[0, t, slot]

        keep() if merge else pl.when(early)(keep)

    def turn(name, near):
        s, r = int(name[1]), zlow
        if name == "U0":
            return 0
        if near:
            return s + (jnp.minimum(s - 1, 7 - r) if name[0] == "U" else jnp.minimum(s, r))
        if name[0] == "U":
            return s - r - 1 + jnp.maximum(0, s - 8 + r)
        return s - 8 + r + jnp.maximum(0, s - r)

    def names(s):
        return ["U0"] if s == 0 else (["U%d" % s, "D%d" % s] if s < 8 else ["U8"])

    def transfers(step):
        for part in range(PARTS):
            if step == 0:
                for src in range(part * width, (part + 1) * width):
                    for cut in range(2):
                        rows = ups[0].at[src, pl.ds(cut * 32, 32)]
                        pltpu.make_async_copy(rows, rows, a_recv.at[src, cut]).wait()
            for up in (True, False):
                last = 8 if up else 7
                if 0 < step <= last:
                    pl.when(held(step, up))(lambda: ring_copy(step - 1, part, up).wait_recv())
                if step < last:
                    go = passed_on(step, up)
                    if step == 0 and not up:
                        go = jnp.logical_and(go, z > 0)
                    pl.when(go)(lambda: ring_copy(step, part, up).start())
        if step == 0:
            load_sel.wait()
        if step < 8:
            for name in names(step):
                pl.when(in_line(name))(lambda: own_sends(name))
        if step == 0:
            @pl.when(z == 0)
            def _():
                pl.semaphore_wait(ready, 1)
                for part in range(PARTS):
                    ring_copy(0, part, False).start()
        if step > 0:
            for name in names(step - 1):
                pl.when(in_line(name))(lambda: picks(name, turn(name, True), False))
            for name in names(step):
                pl.when(jnp.logical_and(late, jnp.logical_not(in_line(name))))(
                    lambda: picks(name, turn(name, False), True)
                )

    def scores_of(q, keys):
        return lax.dot_general(
            q, keys, (((1,), (1,)), ((), ())), preferred_element_type=jnp.float32
        )

    def absorb(rows, scores, values):
        weights = jnp.exp2(scores * FACTOR).astype(jnp.bfloat16)
        acc[rows] += jnp.dot(weights, values, preferred_element_type=jnp.float32)

    def keep_own(kv):
        return pltpu.make_async_copy(nat.at[kv], own_hbm.at[kv], w_sem.at[kv, 8])

    def keep_round(kv, t):
        return pltpu.make_async_copy(land.at[kv, t], kv_hbm.at[kv, t], w_sem.at[kv, t])

    def settle_own():
        for i in range(1, 8):
            src = (pair + 8 - i) % 8
            rows = land0.at[src % 2, src // 2]
            pltpu.make_async_copy(rows, rows, o_recv.at[i - 1]).wait()
        for src in range(4):
            for part in range(2):
                origin = (src + 8 - x - 2 * part) % 4

                def settle(zpos, _):
                    start = pl.multiple_of(zpos * 64 + part * 32, 32)
                    there = pl.multiple_of(origin * 512 + zpos * 64 + part * 32, 32)
                    for kv in range(2):
                        nat[kv, pl.ds(there, 32)] = land0[kv, src, pl.ds(start, 32)]
                    return 0

                lax.fori_loop(0, 8, settle, 0)
        for kv in range(2):
            keep_own(kv).start()

    def own_block(tiles):
        for tile in tiles:
            rows = pl.ds(tile * TILE, TILE)
            count = (tile + 1) * TILE
            scores = scores_of(q_ref[rows], nat[0, :count])
            row_ids = lax.broadcasted_iota(jnp.int32, (TILE, TILE), 0)
            col_ids = lax.broadcasted_iota(jnp.int32, (TILE, TILE), 1)
            edge = jnp.where(col_ids <= row_ids, scores[:, count - TILE:], -1e30)
            scores = jnp.concatenate([scores[:, :count - TILE], edge], axis=1) if tile else edge
            values = nat[1, :count]
            absorb(rows, scores, jnp.concatenate([values, jnp.ones_like(values)], axis=1))

    def wait_round(t):
        for i in range(1, 8):
            src = (pair + 8 - i) % 8
            rows = land.at[src % 2, t, :, src // 2]
            pltpu.make_async_copy(rows, rows, c_recv.at[i, t]).wait()
        for kv in range(2):
            keep_round(kv, t).start()

    def rounds(first_of, count, base, tiles):

        @pl.when(ctx > 0)
        def _():
            size = 512 * count
            slots = lax.broadcasted_iota(jnp.int32, (2 * count, 256, DH), 0).reshape(size, DH) % 2
            live = jnp.where(slots == 0, sel_ref[1, ctx], sel_ref[2, ctx]) >= 0
            ones = jnp.where(live, 1.0, 0.0).astype(jnp.bfloat16)
            keys = land[0, pl.ds(first_of, count)].reshape(size, DH)
            values = land[1, pl.ds(first_of, count)].reshape(size, DH)
            values = jnp.concatenate([values * ones, ones], axis=1)
            for tile in range(tiles):
                rows = pl.ds(pl.multiple_of((base + tile) * TILE, TILE), TILE)
                absorb(rows, scores_of(q_ref[rows], keys), values)

    own_turn = 2 * jnp.where(late, jnp.maximum(zlow, 7 - zlow) - 4, 3)

    start = jnp.where(own_turn >= 4, 3, 4)

    def unit(u):
        @pl.when(u == own_turn)
        def _():
            settle_own()
            own_block(range(6))

        pl.when(u == own_turn + 1)(lambda: own_block(range(6, 8)))

        @pl.when(jnp.logical_and(u < 8, jnp.logical_or(u < own_turn, u > own_turn + 1)))
        def _():
            v = jnp.where(u < own_turn, u, u - 2)

            @pl.when(v % 2 == 0)
            def _():
                wait_round(v)
                wait_round(v + 1)

            rounds(v // 2 * 2, 2, v % 2 * 4, 4)

        @pl.when(u >= 8)
        def _():
            wait_round(u - 2)
            rounds(u - 2, 1, 0, 8)

    def turns(n, _):
        for step in range(9):
            pl.when(n == step)(functools.partial(transfers, step))

        @pl.when(n == 0)
        def _():
            load_q.wait()
            acc[...] = jnp.zeros_like(acc)

        pl.when(jnp.logical_and(n >= start, n < start + 10))(lambda: unit(n - start))
        return 0

    lax.fori_loop(0, 14, turns, 0)
    bad_ref[...] = jnp.zeros_like(bad_ref)
    for tile in range(BLOCK // TILE):
        rows = pl.ds(tile * TILE, TILE)
        mass = acc[rows, DH:]
        out_ref[rows] = (acc[rows, :DH] / mass).astype(out_ref.dtype)
        fine = jnp.logical_and(mass > LEAST, mass < MOST)
        marks = jnp.where(fine, 0.0, 1.0).reshape(TILE // 8, 8, DH)
        bad_ref[...] = jnp.maximum(bad_ref[...], jnp.max(marks, axis=0))

    for kv in range(2):
        keep_own(kv).wait()
        for t in range(8):
            keep_round(kv, t).wait()
    first(False)
    for step in range(8):
        for up in (True, False):
            if up or step < 7:
                @pl.when(passed_on(step, up))
                def _():
                    for part in range(PARTS):
                        ring_copy(step, part, up).wait_send()
    for i in range(1, 8):
        pltpu.make_async_copy(land0.at[0, 0], land0.at[0, 0], o_send.at[i - 1]).wait()
        for t in range(8):
            picked_copy(i, t).wait_send()


def fused(query_rows, key_rows, value_rows, selection):
    dma = pltpu.SemaphoreType.DMA
    anywhere = pl.BlockSpec(memory_space=pl.ANY)
    bf16 = jnp.bfloat16
    return pl.pallas_call(
        fused_kernel,
        out_shape=(
            jax.ShapeDtypeStruct((BLOCK, DH), bf16),
            jax.ShapeDtypeStruct((8, DH), jnp.float32),
            jax.ShapeDtypeStruct((2, BLOCK, DH), bf16),
            jax.ShapeDtypeStruct((2, 8, 2, 4, 64, DH), bf16),
        ),
        in_specs=[anywhere] * 4,
        out_specs=(
            pl.BlockSpec(memory_space=pltpu.VMEM),
            pl.BlockSpec(memory_space=pltpu.VMEM),
            anywhere,
            anywhere,
        ),
        scratch_shapes=[pltpu.VMEM((8, 64, DH), bf16)] * 16 + [
            pltpu.SMEM((SLOTS, 16), jnp.int32),
            pltpu.VMEM((BLOCK, DH), bf16),
            pltpu.VMEM((8, 8, 2, 64, DH), bf16),
            pltpu.VMEM((2, 4, 512, DH), bf16),
            pltpu.VMEM((2, 8, 2, 4, 64, DH), bf16),
            pltpu.VMEM((2, BLOCK, DH), bf16),
            pltpu.VMEM((BLOCK, 2 * DH), jnp.float32),
            dma((2,)), dma((2, 9)),
            dma((2, 4, 2)), dma((8, 2)),
            dma((8, PARTS)), dma((8, PARTS)), dma((8, PARTS)), dma((8, PARTS)),
            dma((7,)), dma((7,)), dma((8, 8)), dma((8, 8)),
            pltpu.SemaphoreType.REGULAR,
        ],
        compiler_params=pltpu.CompilerParams(
            collective_id=0, has_side_effects=True, vmem_limit_bytes=60 * 2**20
        ),
        name="block_attention",
    )(selection.T, query_rows, key_rows, value_rows)


def finish_kernel(
    fast_ref, bad_ref, sel_hbm, q_hbm, own_hbm, kv_hbm, out_ref, sel_ref, q_ref, own, kv, acc, sem
):
    ctx = lax.axis_index("ctx")
    step = pl.program_id(0)
    size = fast_ref.shape[0]
    marked = jnp.max(bad_ref[...]) > 0.0

    @pl.when(jnp.logical_not(marked))
    def _():
        out_ref[...] = fast_ref[...]

    @pl.when(jnp.logical_and(marked, step == 0))
    def _():
        pairs = ((sel_hbm, sel_ref), (q_hbm, q_ref), (own_hbm, own), (kv_hbm, kv))
        copies = [pltpu.make_async_copy(a, b, sem.at[i]) for i, (a, b) in enumerate(pairs)]
        for copy in copies:
            copy.start()
        for copy in copies:
            copy.wait()

    @pl.when(marked)
    def _():
        q = q_ref[pl.ds(pl.multiple_of(step * size, size), size)]
        acc[...] = jnp.zeros_like(acc)

        def absorb(keys, values, allowed, peak):
            scores = lax.dot_general(
                q, keys, (((1,), (1,)), ((), ())), preferred_element_type=jnp.float32
            )
            scores = jnp.where(allowed, scores, -1e30)
            top = jnp.maximum(peak, jnp.max(scores, axis=1, keepdims=True))
            weights = jnp.where(allowed, jnp.exp2((scores - top[:, :1]) * FACTOR), 0.0)
            before = jnp.exp2((peak - top) * FACTOR)[:, :1]
            wide = jnp.concatenate([values, jnp.ones_like(values)], axis=1)
            acc[...] = acc[...] * before + jnp.dot(
                weights.astype(jnp.bfloat16), wide, preferred_element_type=jnp.float32
            )
            return top

        row_ids = lax.broadcasted_iota(jnp.int32, (size, 512), 0) + step * size
        col_ids = lax.broadcasted_iota(jnp.int32, (size, 512), 1)

        def own_part(i, peak):
            there = pl.ds(pl.multiple_of(i * 512, 512), 512)
            return absorb(own[0, there], own[1, there], col_ids + i * 512 <= row_ids, peak)

        def round_part(t, peak):
            live = jnp.where(col_ids < 256, sel_ref[1, ctx], sel_ref[2, ctx]) >= 0
            return absorb(kv[0, t].reshape(512, DH), kv[1, t].reshape(512, DH), live, peak)

        peak = jnp.full((size, DH), -1e30, jnp.float32)
        peak = lax.fori_loop(0, (step + 1) * size // 512, own_part, peak)
        lax.fori_loop(0, 8, round_part, peak)
        out_ref[...] = (acc[:, :DH] / acc[:, DH:]).astype(out_ref.dtype)


def attention(query_rows, key_rows, value_rows, selection):
    fast, bad, own, kv = fused(query_rows, key_rows, value_rows, selection)
    anywhere = pl.BlockSpec(memory_space=pl.ANY)
    size = 1024
    return pl.pallas_call(
        finish_kernel,
        out_shape=jax.ShapeDtypeStruct(fast.shape, fast.dtype),
        grid=(BLOCK // size,),
        in_specs=[
            pl.BlockSpec((size, DH), lambda i: (i, 0)),
            pl.BlockSpec((8, DH), lambda i: (0, 0)),
            anywhere, anywhere, anywhere, anywhere,
        ],
        out_specs=pl.BlockSpec((size, DH), lambda i: (i, 0)),
        scratch_shapes=[
            pltpu.SMEM((SLOTS, 16), jnp.int32),
            pltpu.VMEM((BLOCK, DH), jnp.bfloat16),
            pltpu.VMEM((2, BLOCK, DH), jnp.bfloat16),
            pltpu.VMEM((2, 8, 2, 4, 64, DH), jnp.bfloat16),
            pltpu.VMEM((size, 2 * DH), jnp.float32),
            pltpu.SemaphoreType.DMA((4,)),
        ],
        compiler_params=pltpu.CompilerParams(vmem_limit_bytes=60 * 2**20),
        name="finish",
    )(fast, bad, selection.T, query_rows, own, kv)


def solution(mesh):
    placed = (P("ctx", "head"), P(("ctx", "head"), None), P(("ctx", "head"), None), P())
    return jax.shard_map(
        attention, mesh=mesh, in_specs=placed, out_specs=P("ctx", "head"), check_vma=False
    )
```

```python
import functools

import jax
import jax.numpy as jnp
from jax import lax
from jax.experimental import pallas as pl
from jax.experimental.pallas import tpu as pltpu
from jax.sharding import PartitionSpec as P

DH = 128
BLOCK = 2048
SLOTS = 3
PARTS = 4
TILE = 256
MESH = pl.DeviceIdType.MESH
FACTOR = DH**-0.5 * 1.4426950408889634
START = 6
LEAST, MOST = 2.0**-80, 2.0**100


def place():
    ctx = lax.axis_index("ctx")
    head = lax.axis_index("head")
    half, pair = ctx // 8, ctx % 8
    y, zlow = head // 8, head % 8
    return half, pair // 2, pair % 2, y, zlow


def device(half, pair, y, zlow):
    return (half * 8 + pair, y * 8 + zlow)


def fused_kernel(sel_hbm, q_hbm, k_hbm, v_hbm, out_ref, bad_ref, own_hbm, kv_hbm, *scratch):
    ups, downs = scratch[:9], scratch[9:16]
    (sel_ref, q_ref, picked, land0, land, nat, acc, l_sem, w_sem,
     a_send, a_recv, up_send, up_recv, down_send, down_recv,
     o_send, o_recv, c_send, c_recv, ready) = scratch[16:]
    half, x, core, y, zlow = place()
    ctx = lax.axis_index("ctx")
    pair = x * 2 + core
    z = half * 8 + zlow
    above, below = (z + 1) % 16, (z + 15) % 16
    early, late = half == 0, half == 1

    def buffer(name):
        return ups[int(name[1])] if name[0] == "U" else downs[int(name[1]) - 1]

    def in_line(name):
        s = int(name[1])
        return zlow >= s if name[0] == "U" else zlow + s < 8

    load_sel = pltpu.make_async_copy(sel_hbm, sel_ref, l_sem.at[0])
    load_sel.start()

    barrier = pltpu.get_barrier_semaphore()

    def hello(target):
        pl.semaphore_signal(barrier, inc=1, device_id=target, device_id_type=MESH)

    for src in range(8):
        for part in range(2):
            origin = (x + 8 - src // 2 - 2 * part) % 4

            @pl.when(jnp.logical_or(src != pair, origin != y))
            def _():
                hello(device(half, src, origin, zlow))
    pl.when(z < 15)(lambda: hello(device(above // 8, pair, y, above % 8)))
    hello(device(below // 8, pair, y, below % 8))
    for i in range(1, 8):
        hello(device(half, (pair + i) % 8, y, zlow))
    pl.semaphore_wait(barrier, 25 - jnp.where(y % 2 == 0, 1, 0) - jnp.where(z == 0, 1, 0))

    @pl.when(z == 15)
    def _():
        pl.semaphore_signal(ready, inc=1, device_id=device(0, pair, y, 0), device_id_type=MESH)

    def first(act):
        for head in range(4):
            for part in range(2):
                for kv, rows in ((0, k_hbm), (1, v_hbm)):
                    mine = jnp.logical_and(
                        (y + 2 * part) % 4 == 0, jnp.logical_and(core == kv, head == y)
                    )
                    src = rows.at[pl.ds(part * 32, 32), pl.ds(head * DH, DH)]
                    dst = ups[0].at[pair, pl.ds(part * 32, 32)]

                    @pl.when(jnp.logical_not(mine))
                    def _():
                        copy = pltpu.make_async_remote_copy(
                            src_ref=src,
                            dst_ref=dst,
                            send_sem=a_send.at[kv, head, part],
                            recv_sem=a_recv.at[pair, part],
                            device_id=device(half, (x + y + 2 * part) % 4 * 2 + kv, head, zlow),
                            device_id_type=MESH,
                        )
                        copy.start() if act else copy.wait_send()

                    if act:
                        @pl.when(mine)
                        def _():
                            pltpu.make_async_copy(src, dst, a_recv.at[pair, part]).start()

    first(True)
    load_q = pltpu.make_async_copy(q_hbm, q_ref, l_sem.at[1])
    load_q.start()

    width = 8 // PARTS

    def ring_copy(step, part, up):
        bufs = ups if up else (ups[0],) + tuple(downs)
        to = above if up else below
        return pltpu.make_async_remote_copy(
            src_ref=bufs[step].at[pl.ds(part * width, width)],
            dst_ref=bufs[step + 1].at[pl.ds(part * width, width)],
            send_sem=(up_send if up else down_send).at[step],
            recv_sem=(up_recv if up else down_recv).at[step, part],
            device_id=device(to // 8, pair, y, to % 8),
            device_id_type=MESH,
        )

    def held(step, up):
        return jnp.logical_or(late, in_line(("U" if up else "D") + str(step)))

    def passed_on(step, up):
        edge = zlow == (7 if up else 0)
        return jnp.logical_and(held(step, up), jnp.logical_not(jnp.logical_and(late, edge)))

    def own_sends(name):
        buf = buffer(name)
        s = int(name[1])
        zpos = zlow - s if name[0] == "U" else zlow + s
        rows = pl.ds(pl.multiple_of(zpos * 64, 64), 64)
        for i in (4, 3, 5, 2, 6, 1, 7):
            target = (pair + i) % 8
            pltpu.make_async_remote_copy(
                src_ref=buf.at[target],
                dst_ref=land0.at[core, x, rows],
                send_sem=o_send.at[i - 1],
                recv_sem=o_recv.at[i - 1],
                device_id=device(half, target, y, zlow),
                device_id_type=MESH,
            ).start()
        land0[core, x, rows] = buf[pair]

    def picked_copy(i, t):
        return pltpu.make_async_remote_copy(
            src_ref=picked.at[i, t],
            dst_ref=land.at[core, t, :, x],
            send_sem=c_send.at[i],
            recv_sem=c_recv.at[i, t],
            device_id=device(half, (pair + i) % 8, y, zlow),
            device_id_type=MESH,
        )

    def block_for(row, slot):
        block = sel_ref[slot + 1, row]
        return jnp.maximum(jnp.where(block < 0, sel_ref[2 - slot, row], block), 0)

    def picks(name, t, merge):
        def to(n, _):
            i = (n + 4) % 8
            for slot in range(2):
                block = block_for(half * 8 + (pair + i) % 8, slot)
                rows = buffer(name)[block % 8]
                if merge:
                    rows = jnp.where(block < 8, rows, picked[i, t, slot])
                picked[i, t, slot] = rows
            if merge:
                pl.when(i > 0)(lambda: picked_copy(i, t).start())
            else:
                pl.when(jnp.logical_and(early, i > 0))(lambda: picked_copy(i, t).start())
            return 0

        lax.fori_loop(0, 8, to, 0)

        def keep():
            for slot in range(2):
                land[core, t, slot, x] = picked[0, t, slot]

        keep() if merge else pl.when(early)(keep)

    def turn(name, near):
        s, r = int(name[1]), zlow
        if name == "U0":
            return 0
        if near:
            return s + (jnp.minimum(s - 1, 7 - r) if name[0] == "U" else jnp.minimum(s, r))
        if name[0] == "U":
            return s - r - 1 + jnp.maximum(0, s - 8 + r)
        return s - 8 + r + jnp.maximum(0, s - r)

    def names(s):
        return ["U0"] if s == 0 else (["U%d" % s, "D%d" % s] if s < 8 else ["U8"])

    def transfers(step):
        for part in range(PARTS):
            if step == 0:
                for src in range(part * width, (part + 1) * width):
                    for cut in range(2):
                        rows = ups[0].at[src, pl.ds(cut * 32, 32)]
                        pltpu.make_async_copy(rows, rows, a_recv.at[src, cut]).wait()
            for up in (True, False):
                last = 8 if up else 7
                if 0 < step <= last:
                    pl.when(held(step, up))(lambda: ring_copy(step - 1, part, up).wait_recv())
                if step < last:
                    go = passed_on(step, up)
                    if step == 0 and not up:
                        go = jnp.logical_and(go, z > 0)
                    pl.when(go)(lambda: ring_copy(step, part, up).start())
        if step == 0:
            load_sel.wait()
        if step < 8:
            for name in names(step):
                pl.when(in_line(name))(lambda: own_sends(name))
        if step == 0:
            @pl.when(z == 0)
            def _():
                pl.semaphore_wait(ready, 1)
                for part in range(PARTS):
                    ring_copy(0, part, False).start()
        for name in (names(step) if step < 4 else []) + (names(step - 1) if step > 4 else []):
            pl.when(in_line(name))(lambda: picks(name, turn(name, True), False))
        if step > 0:
            for name in names(step):
                pl.when(jnp.logical_and(late, jnp.logical_not(in_line(name))))(
                    lambda: picks(name, turn(name, False), True)
                )

    def scores_of(q, keys):
        return lax.dot_general(
            q, keys, (((1,), (1,)), ((), ())), preferred_element_type=jnp.float32
        )

    def absorb(rows, scores, values):
        weights = jnp.exp2(scores * FACTOR).astype(jnp.bfloat16)
        acc[rows] += jnp.dot(weights, values, preferred_element_type=jnp.float32)

    def keep_own(kv):
        return pltpu.make_async_copy(nat.at[kv], own_hbm.at[kv], w_sem.at[kv, 8])

    def keep_round(kv, t):
        return pltpu.make_async_copy(land.at[kv, t], kv_hbm.at[kv, t], w_sem.at[kv, t])

    def settle_own():
        for i in range(1, 8):
            src = (pair + 8 - i) % 8
            rows = land0.at[src % 2, src // 2]
            pltpu.make_async_copy(rows, rows, o_recv.at[i - 1]).wait()
        for src in range(4):
            for part in range(2):
                origin = (src + 8 - x - 2 * part) % 4

                def settle(zpos, _):
                    start = pl.multiple_of(zpos * 64 + part * 32, 32)
                    there = pl.multiple_of(origin * 512 + zpos * 64 + part * 32, 32)
                    for kv in range(2):
                        nat[kv, pl.ds(there, 32)] = land0[kv, src, pl.ds(start, 32)]
                    return 0

                lax.fori_loop(0, 8, settle, 0)
        for kv in range(2):
            keep_own(kv).start()

    def own_block(tiles):
        for tile in tiles:
            rows = pl.ds(tile * TILE, TILE)
            count = (tile + 1) * TILE
            scores = scores_of(q_ref[rows], nat[0, :count])
            row_ids = lax.broadcasted_iota(jnp.int32, (TILE, TILE), 0)
            col_ids = lax.broadcasted_iota(jnp.int32, (TILE, TILE), 1)
            edge = jnp.where(col_ids <= row_ids, scores[:, count - TILE:], -1e30)
            scores = jnp.concatenate([scores[:, :count - TILE], edge], axis=1) if tile else edge
            values = nat[1, :count]
            absorb(rows, scores, jnp.concatenate([values, jnp.ones_like(values)], axis=1))

    def wait_round(t):
        for i in range(1, 8):
            src = (pair + 8 - i) % 8
            rows = land.at[src % 2, t, :, src // 2]
            pltpu.make_async_copy(rows, rows, c_recv.at[i, t]).wait()
        for kv in range(2):
            keep_round(kv, t).start()

    def rounds(first_of, count, base, tiles):

        @pl.when(ctx > 0)
        def _():
            size = 512 * count
            slots = lax.broadcasted_iota(jnp.int32, (2 * count, 256, DH), 0).reshape(size, DH) % 2
            live = jnp.where(slots == 0, sel_ref[1, ctx], sel_ref[2, ctx]) >= 0
            ones = jnp.where(live, 1.0, 0.0).astype(jnp.bfloat16)
            keys = land[0, pl.ds(first_of, count)].reshape(size, DH)
            values = land[1, pl.ds(first_of, count)].reshape(size, DH)
            values = jnp.concatenate([values * ones, ones], axis=1)
            for tile in range(tiles):
                rows = pl.ds(pl.multiple_of((base + tile) * TILE, TILE), TILE)
                absorb(rows, scores_of(q_ref[rows], keys), values)

    own_turn = 2 * jnp.where(late, jnp.maximum(zlow, 7 - zlow) - 4, 3)


    def unit(u):
        @pl.when(u == own_turn)
        def _():
            settle_own()
            own_block(range(6))

        pl.when(u == own_turn + 1)(lambda: own_block(range(6, 8)))

        @pl.when(jnp.logical_and(u < 8, jnp.logical_or(u < own_turn, u > own_turn + 1)))
        def _():
            v = jnp.where(u < own_turn, u, u - 2)

            @pl.when(v % 2 == 0)
            def _():
                wait_round(v)
                wait_round(v + 1)

            rounds(v // 2 * 2, 2, v % 2 * 4, 4)

        @pl.when(u >= 8)
        def _():
            wait_round(u - 2)
            rounds(u - 2, 1, 0, 8)

    def sent():
        first(False)
        for step in range(8):
            for up in (True, False):
                if up or step < 7:
                    piece = (ups if up else (ups[0],) + tuple(downs))[step]
                    semaphore = (up_send if up else down_send).at[step]
                    pl.when(passed_on(step, up))(
                        lambda: pltpu.make_async_copy(piece, piece, semaphore).wait()
                    )
        for i in range(1, 8):
            pltpu.make_async_copy(land0.at[0, 0], land0.at[0, 0], o_send.at[i - 1]).wait()

    def turns(n, _):
        for step in range(9):
            pl.when(n == step)(functools.partial(transfers, step))

        @pl.when(n == 0)
        def _():
            load_q.wait()
            acc[...] = jnp.zeros_like(acc)

        pl.when(n == START + 7)(sent)
        pl.when(n >= START)(lambda: unit(n - START))
        return 0

    lax.fori_loop(0, START + 10, turns, 0)
    bad_ref[...] = jnp.zeros_like(bad_ref)
    for tile in range(BLOCK // TILE):
        rows = pl.ds(tile * TILE, TILE)
        mass = acc[rows, DH:]
        out_ref[rows] = (acc[rows, :DH] / mass).astype(out_ref.dtype)
        fine = jnp.logical_and(mass > LEAST, mass < MOST)
        marks = jnp.where(fine, 0.0, 1.0).reshape(TILE // 8, 8, DH)
        bad_ref[...] = jnp.maximum(bad_ref[...], jnp.max(marks, axis=0))

    for kv in range(2):
        keep_own(kv).wait()
        for t in range(8):
            keep_round(kv, t).wait()
    for i in range(1, 8):
        pltpu.make_async_copy(picked.at[i], picked.at[i], c_send.at[i]).wait()


def fused(query_rows, key_rows, value_rows, selection):
    dma = pltpu.SemaphoreType.DMA
    anywhere = pl.BlockSpec(memory_space=pl.ANY)
    bf16 = jnp.bfloat16
    return pl.pallas_call(
        fused_kernel,
        out_shape=(
            jax.ShapeDtypeStruct((BLOCK, DH), bf16),
            jax.ShapeDtypeStruct((8, DH), jnp.float32),
            jax.ShapeDtypeStruct((2, BLOCK, DH), bf16),
            jax.ShapeDtypeStruct((2, 8, 2, 4, 64, DH), bf16),
        ),
        in_specs=[anywhere] * 4,
        out_specs=(
            pl.BlockSpec(memory_space=pltpu.VMEM),
            pl.BlockSpec(memory_space=pltpu.VMEM),
            anywhere,
            anywhere,
        ),
        scratch_shapes=[pltpu.VMEM((8, 64, DH), bf16)] * 16 + [
            pltpu.SMEM((SLOTS, 16), jnp.int32),
            pltpu.VMEM((BLOCK, DH), bf16),
            pltpu.VMEM((8, 8, 2, 64, DH), bf16),
            pltpu.VMEM((2, 4, 512, DH), bf16),
            pltpu.VMEM((2, 8, 2, 4, 64, DH), bf16),
            pltpu.VMEM((2, BLOCK, DH), bf16),
            pltpu.VMEM((BLOCK, 2 * DH), jnp.float32),
            dma((2,)), dma((2, 9)),
            dma((2, 4, 2)), dma((8, 2)),
            dma((8,)), dma((8, PARTS)), dma((8,)), dma((8, PARTS)),
            dma((7,)), dma((7,)), dma((8,)), dma((8, 8)),
            pltpu.SemaphoreType.REGULAR,
        ],
        compiler_params=pltpu.CompilerParams(
            collective_id=0, has_side_effects=True, vmem_limit_bytes=60 * 2**20
        ),
        name="block_attention",
    )(selection.T, query_rows, key_rows, value_rows)


def finish_kernel(
    fast_ref, bad_ref, sel_hbm, q_hbm, own_hbm, kv_hbm, out_ref, sel_ref, q_ref, own, kv, acc, sem
):
    ctx = lax.axis_index("ctx")
    step = pl.program_id(0)
    size = fast_ref.shape[0]
    marked = jnp.max(bad_ref[...]) > 0.0

    @pl.when(jnp.logical_not(marked))
    def _():
        out_ref[...] = fast_ref[...]

    @pl.when(jnp.logical_and(marked, step == 0))
    def _():
        pairs = ((sel_hbm, sel_ref), (q_hbm, q_ref), (own_hbm, own), (kv_hbm, kv))
        copies = [pltpu.make_async_copy(a, b, sem.at[i]) for i, (a, b) in enumerate(pairs)]
        for copy in copies:
            copy.start()
        for copy in copies:
            copy.wait()

    @pl.when(marked)
    def _():
        q = q_ref[pl.ds(pl.multiple_of(step * size, size), size)]
        acc[...] = jnp.zeros_like(acc)

        def absorb(keys, values, allowed, peak):
            scores = lax.dot_general(
                q, keys, (((1,), (1,)), ((), ())), preferred_element_type=jnp.float32
            )
            scores = jnp.where(allowed, scores, -1e30)
            top = jnp.maximum(peak, jnp.max(scores, axis=1, keepdims=True))
            weights = jnp.where(allowed, jnp.exp2((scores - top[:, :1]) * FACTOR), 0.0)
            before = jnp.exp2((peak - top) * FACTOR)[:, :1]
            wide = jnp.concatenate([values, jnp.ones_like(values)], axis=1)
            acc[...] = acc[...] * before + jnp.dot(
                weights.astype(jnp.bfloat16), wide, preferred_element_type=jnp.float32
            )
            return top

        row_ids = lax.broadcasted_iota(jnp.int32, (size, 512), 0) + step * size
        col_ids = lax.broadcasted_iota(jnp.int32, (size, 512), 1)

        def own_part(i, peak):
            there = pl.ds(pl.multiple_of(i * 512, 512), 512)
            return absorb(own[0, there], own[1, there], col_ids + i * 512 <= row_ids, peak)

        def round_part(t, peak):
            live = jnp.where(col_ids < 256, sel_ref[1, ctx], sel_ref[2, ctx]) >= 0
            return absorb(kv[0, t].reshape(512, DH), kv[1, t].reshape(512, DH), live, peak)

        peak = jnp.full((size, DH), -1e30, jnp.float32)
        peak = lax.fori_loop(0, (step + 1) * size // 512, own_part, peak)
        lax.fori_loop(0, 8, round_part, peak)
        out_ref[...] = (acc[:, :DH] / acc[:, DH:]).astype(out_ref.dtype)


def attention(query_rows, key_rows, value_rows, selection):
    fast, bad, own, kv = fused(query_rows, key_rows, value_rows, selection)
    anywhere = pl.BlockSpec(memory_space=pl.ANY)
    size = 1024
    return pl.pallas_call(
        finish_kernel,
        out_shape=jax.ShapeDtypeStruct(fast.shape, fast.dtype),
        grid=(BLOCK // size,),
        in_specs=[
            pl.BlockSpec((size, DH), lambda i: (i, 0)),
            pl.BlockSpec((8, DH), lambda i: (0, 0)),
            anywhere, anywhere, anywhere, anywhere,
        ],
        out_specs=pl.BlockSpec((size, DH), lambda i: (i, 0)),
        scratch_shapes=[
            pltpu.SMEM((SLOTS, 16), jnp.int32),
            pltpu.VMEM((BLOCK, DH), jnp.bfloat16),
            pltpu.VMEM((2, BLOCK, DH), jnp.bfloat16),
            pltpu.VMEM((2, 8, 2, 4, 64, DH), jnp.bfloat16),
            pltpu.VMEM((size, 2 * DH), jnp.float32),
            pltpu.SemaphoreType.DMA((4,)),
        ],
        compiler_params=pltpu.CompilerParams(vmem_limit_bytes=60 * 2**20),
        name="finish",
    )(fast, bad, selection.T, query_rows, own, kv)


def solution(mesh):
    placed = (P("ctx", "head"), P(("ctx", "head"), None), P(("ctx", "head"), None), P())
    return jax.shard_map(
        attention, mesh=mesh, in_specs=placed, out_specs=P("ctx", "head"), check_vma=False
    )
```

```python
import functools

import jax
import jax.numpy as jnp
from jax import lax
from jax.experimental import pallas as pl
from jax.experimental.pallas import tpu as pltpu
from jax.sharding import PartitionSpec as P

DH = 128
BLOCK = 2048
SLOTS = 3
PARTS = 4
TILE = 256
MESH = pl.DeviceIdType.MESH
FACTOR = DH**-0.5 * 1.4426950408889634
START = 6
LEAST, MOST = 2.0**-80, 2.0**100


def place():
    ctx = lax.axis_index("ctx")
    head = lax.axis_index("head")
    half, pair = ctx // 8, ctx % 8
    y, zlow = head // 8, head % 8
    return half, pair // 2, pair % 2, y, zlow


def device(half, pair, y, zlow):
    return (half * 8 + pair, y * 8 + zlow)


def fused_kernel(sel_hbm, q_hbm, k_hbm, v_hbm, out_hbm, bad_ref, own_hbm, kv_hbm, *scratch):
    ups, downs = scratch[:9], scratch[9:16]
    (sel_ref, q_ref, k_ref, v_ref, out_ref, picked, land0, land, nat, acc, l_sem, w_sem, e_sem,
     a_send, a_recv, up_send, up_recv, down_send, down_recv,
     o_send, o_recv, c_send, c_recv, ready) = scratch[16:]
    half, x, core, y, zlow = place()
    ctx = lax.axis_index("ctx")
    pair = x * 2 + core
    z = half * 8 + zlow
    above, below = (z + 1) % 16, (z + 15) % 16
    early, late = half == 0, half == 1

    def buffer(name):
        return ups[int(name[1])] if name[0] == "U" else downs[int(name[1]) - 1]

    def in_line(name):
        s = int(name[1])
        return zlow >= s if name[0] == "U" else zlow + s < 8

    load_sel = pltpu.make_async_copy(sel_hbm, sel_ref, l_sem.at[0])
    load_sel.start()
    load_rows = [
        pltpu.make_async_copy(k_hbm, k_ref, l_sem.at[2]),
        pltpu.make_async_copy(v_hbm, v_ref, l_sem.at[3]),
    ]
    for load in load_rows:
        load.start()

    barrier = pltpu.get_barrier_semaphore()

    def hello(target):
        pl.semaphore_signal(barrier, inc=1, device_id=target, device_id_type=MESH)

    for src in range(8):
        for part in range(2):
            origin = (x + 8 - src // 2 - 2 * part) % 4

            @pl.when(jnp.logical_or(src != pair, origin != y))
            def _():
                hello(device(half, src, origin, zlow))
    pl.when(z < 15)(lambda: hello(device(above // 8, pair, y, above % 8)))
    hello(device(below // 8, pair, y, below % 8))
    for i in range(1, 8):
        hello(device(half, (pair + i) % 8, y, zlow))
    pl.semaphore_wait(barrier, 25 - jnp.where(y % 2 == 0, 1, 0) - jnp.where(z == 0, 1, 0))

    @pl.when(z == 15)
    def _():
        pl.semaphore_signal(ready, inc=1, device_id=device(0, pair, y, 0), device_id_type=MESH)

    def first(act):
        for head in range(4):
            for part in range(2):
                for kv, rows in ((0, k_ref), (1, v_ref)):
                    mine = jnp.logical_and(
                        (y + 2 * part) % 4 == 0, jnp.logical_and(core == kv, head == y)
                    )
                    src = rows.at[pl.ds(part * 32, 32), pl.ds(head * DH, DH)]
                    dst = ups[0].at[pair, pl.ds(part * 32, 32)]

                    @pl.when(jnp.logical_not(mine))
                    def _():
                        copy = pltpu.make_async_remote_copy(
                            src_ref=src,
                            dst_ref=dst,
                            send_sem=a_send.at[kv, head, part],
                            recv_sem=a_recv.at[pair, part],
                            device_id=device(half, (x + y + 2 * part) % 4 * 2 + kv, head, zlow),
                            device_id_type=MESH,
                        )
                        copy.start() if act else copy.wait_send()

                    if act:
                        @pl.when(mine)
                        def _():
                            pltpu.make_async_copy(src, dst, a_recv.at[pair, part]).start()

    for load in load_rows:
        load.wait()
    first(True)
    load_q = pltpu.make_async_copy(q_hbm, q_ref, l_sem.at[1])
    load_q.start()

    width = 8 // PARTS

    def ring_copy(step, part, up):
        bufs = ups if up else (ups[0],) + tuple(downs)
        to = above if up else below
        return pltpu.make_async_remote_copy(
            src_ref=bufs[step].at[pl.ds(part * width, width)],
            dst_ref=bufs[step + 1].at[pl.ds(part * width, width)],
            send_sem=(up_send if up else down_send).at[step],
            recv_sem=(up_recv if up else down_recv).at[step, part],
            device_id=device(to // 8, pair, y, to % 8),
            device_id_type=MESH,
        )

    def held(step, up):
        return jnp.logical_or(late, in_line(("U" if up else "D") + str(step)))

    def passed_on(step, up):
        edge = zlow == (7 if up else 0)
        return jnp.logical_and(held(step, up), jnp.logical_not(jnp.logical_and(late, edge)))

    def own_sends(name):
        buf = buffer(name)
        s = int(name[1])
        zpos = zlow - s if name[0] == "U" else zlow + s
        rows = pl.ds(pl.multiple_of(zpos * 64, 64), 64)
        for i in (4, 3, 5, 2, 6, 1, 7):
            target = (pair + i) % 8
            pltpu.make_async_remote_copy(
                src_ref=buf.at[target],
                dst_ref=land0.at[core, x, rows],
                send_sem=o_send.at[i - 1],
                recv_sem=o_recv.at[i - 1],
                device_id=device(half, target, y, zlow),
                device_id_type=MESH,
            ).start()
        land0[core, x, rows] = buf[pair]

    def picked_copy(i, t):
        return pltpu.make_async_remote_copy(
            src_ref=picked.at[i, t],
            dst_ref=land.at[core, t, x],
            send_sem=c_send.at[i],
            recv_sem=c_recv.at[i, t],
            device_id=device(half, (pair + i) % 8, y, zlow),
            device_id_type=MESH,
        )

    def block_for(row, slot):
        block = sel_ref[slot + 1, row]
        return jnp.maximum(jnp.where(block < 0, sel_ref[2 - slot, row], block), 0)

    def picks(name, t, merge):
        def to(n, _):
            i = (n + 4) % 8
            for slot in range(2):
                block = block_for(half * 8 + (pair + i) % 8, slot)
                rows = buffer(name)[block % 8]
                if merge:
                    rows = jnp.where(block < 8, rows, picked[i, t, slot])
                picked[i, t, slot] = rows
            if merge:
                pl.when(i > 0)(lambda: picked_copy(i, t).start())
            else:
                pl.when(jnp.logical_and(early, i > 0))(lambda: picked_copy(i, t).start())
            return 0

        lax.fori_loop(0, 8, to, 0)

        def keep():
            for slot in range(2):
                land[core, t, x, slot] = picked[0, t, slot]

        keep() if merge else pl.when(early)(keep)

    def turn(name, near):
        s, r = int(name[1]), zlow
        if name == "U0":
            return 0
        if near:
            return s + (jnp.minimum(s - 1, 7 - r) if name[0] == "U" else jnp.minimum(s, r))
        if name[0] == "U":
            return s - r - 1 + jnp.maximum(0, s - 8 + r)
        return s - 8 + r + jnp.maximum(0, s - r)

    def names(s):
        return ["U0"] if s == 0 else (["U%d" % s, "D%d" % s] if s < 8 else ["U8"])

    def transfers(step):
        for part in range(PARTS):
            if step == 0:
                for src in range(part * width, (part + 1) * width):
                    for cut in range(2):
                        rows = ups[0].at[src, pl.ds(cut * 32, 32)]
                        pltpu.make_async_copy(rows, rows, a_recv.at[src, cut]).wait()
            for up in (True, False):
                last = 8 if up else 7
                if 0 < step <= last:
                    pl.when(held(step, up))(lambda: ring_copy(step - 1, part, up).wait_recv())
                if step < last:
                    go = passed_on(step, up)
                    if step == 0 and not up:
                        go = jnp.logical_and(go, z > 0)
                    pl.when(go)(lambda: ring_copy(step, part, up).start())
        if step == 0:
            load_sel.wait()
        if step < 8:
            for name in names(step):
                pl.when(in_line(name))(lambda: own_sends(name))
        if step == 0:
            @pl.when(z == 0)
            def _():
                pl.semaphore_wait(ready, 1)
                for part in range(PARTS):
                    ring_copy(0, part, False).start()
        for name in (names(step) if step < 4 else []) + (names(step - 1) if step > 4 else []):
            pl.when(in_line(name))(lambda: picks(name, turn(name, True), False))
        if step > 0:
            for name in names(step):
                pl.when(jnp.logical_and(late, jnp.logical_not(in_line(name))))(
                    lambda: picks(name, turn(name, False), True)
                )

    def scores_of(q, keys):
        return lax.dot_general(
            q, keys, (((1,), (1,)), ((), ())), preferred_element_type=jnp.float32
        )

    def absorb(rows, scores, values):
        weights = jnp.exp2(scores * FACTOR).astype(jnp.bfloat16)
        acc[rows] += jnp.dot(weights, values, preferred_element_type=jnp.float32)

    def keep_own(kv):
        return pltpu.make_async_copy(nat.at[kv], own_hbm.at[kv], w_sem.at[kv, 8])

    def keep_round(kv, t):
        return pltpu.make_async_copy(land.at[kv, t], kv_hbm.at[kv, t], w_sem.at[kv, t])

    def settle_own():
        for i in range(1, 8):
            src = (pair + 8 - i) % 8
            rows = land0.at[src % 2, src // 2]
            pltpu.make_async_copy(rows, rows, o_recv.at[i - 1]).wait()
        for src in range(4):
            for part in range(2):
                origin = (src + 8 - x - 2 * part) % 4

                def settle(zpos, _):
                    start = pl.multiple_of(zpos * 64 + part * 32, 32)
                    there = pl.multiple_of(origin * 512 + zpos * 64 + part * 32, 32)
                    for kv in range(2):
                        nat[kv, pl.ds(there, 32)] = land0[kv, src, pl.ds(start, 32)]
                    return 0

                lax.fori_loop(0, 8, settle, 0)
        for kv in range(2):
            keep_own(kv).start()

    def own_block(tiles):
        for tile in tiles:
            rows = pl.ds(tile * TILE, TILE)
            count = (tile + 1) * TILE
            scores = scores_of(q_ref[rows], nat[0, :count])
            row_ids = lax.broadcasted_iota(jnp.int32, (TILE, TILE), 0)
            col_ids = lax.broadcasted_iota(jnp.int32, (TILE, TILE), 1)
            edge = jnp.where(col_ids <= row_ids, scores[:, count - TILE:], -1e30)
            scores = jnp.concatenate([scores[:, :count - TILE], edge], axis=1) if tile else edge
            values = nat[1, :count]
            absorb(rows, scores, jnp.concatenate([values, jnp.ones_like(values)], axis=1))

    def wait_round(t):
        for i in range(1, 8):
            src = (pair + 8 - i) % 8
            rows = land.at[src % 2, t, src // 2]
            pltpu.make_async_copy(rows, rows, c_recv.at[i, t]).wait()
        for kv in range(2):
            keep_round(kv, t).start()

    def operands(first_of, count):
        size = 512 * count
        slots = lax.broadcasted_iota(jnp.int32, (4 * count, 2, 64, DH), 1).reshape(size, DH)
        live = jnp.where(slots == 0, sel_ref[1, ctx], sel_ref[2, ctx]) >= 0
        ones = jnp.where(live, 1.0, 0.0).astype(jnp.bfloat16)
        keys = land[0, pl.ds(first_of, count)].reshape(size, DH)
        values = land[1, pl.ds(first_of, count)].reshape(size, DH)
        return keys, jnp.concatenate([values * ones, ones], axis=1)

    def rounds(first_of, count, base, tiles):
        @pl.when(ctx > 0)
        def _():
            keys, values = operands(first_of, count)
            for tile in range(tiles):
                rows = pl.ds(pl.multiple_of((base + tile) * TILE, TILE), TILE)
                absorb(rows, scores_of(q_ref[rows], keys), values)

    own_turn = 2 * jnp.where(late, jnp.maximum(zlow, 7 - zlow) - 4, 3)


    def unit(u):
        @pl.when(u == own_turn)
        def _():
            settle_own()
            own_block(range(6))

        pl.when(u == own_turn + 1)(lambda: own_block(range(6, 8)))

        @pl.when(jnp.logical_and(u < 8, jnp.logical_or(u < own_turn, u > own_turn + 1)))
        def _():
            v = jnp.where(u < own_turn, u, u - 2)

            @pl.when(v % 2 == 0)
            def _():
                wait_round(v)
                wait_round(v + 1)

            rounds(v // 2 * 2, 2, v % 2 * 4, 4)

        @pl.when(u == 8)
        def _():
            wait_round(6)
            rounds(6, 1, 0, 8)

    def sent():
        first(False)
        for step in range(8):
            for up in (True, False):
                if up or step < 7:
                    piece = (ups if up else (ups[0],) + tuple(downs))[step]
                    semaphore = (up_send if up else down_send).at[step]
                    pl.when(passed_on(step, up))(
                        lambda: pltpu.make_async_copy(piece, piece, semaphore).wait()
                    )
        for i in range(1, 8):
            pltpu.make_async_copy(land0.at[0, 0], land0.at[0, 0], o_send.at[i - 1]).wait()

    def turns(n, _):
        for step in range(9):
            pl.when(n == step)(functools.partial(transfers, step))

        @pl.when(n == 0)
        def _():
            load_q.wait()
            acc[...] = jnp.zeros_like(acc)

        pl.when(n == START + 7)(sent)
        begun = n - START + jnp.where(z == 0, 1, 0)
        pl.when(jnp.logical_and(begun >= 0, begun < 9))(lambda: unit(begun))
        return 0

    lax.fori_loop(0, START + 9, turns, 0)
    bad_ref[...] = jnp.zeros_like(bad_ref)
    wait_round(7)
    keys, values = operands(7, 1)
    results = []
    for tile in range(BLOCK // TILE):
        rows = pl.ds(tile * TILE, TILE)
        weights = jnp.exp2(scores_of(q_ref[rows], keys) * FACTOR).astype(jnp.bfloat16)
        total = acc[rows] + jnp.dot(weights, values, preferred_element_type=jnp.float32)
        mass = total[:, DH:]
        out_ref[rows] = (total[:, :DH] / mass).astype(out_ref.dtype)
        fine = jnp.logical_and(mass > LEAST, mass < MOST)
        marks = jnp.where(fine, 0.0, 1.0).reshape(TILE // 8, 8, DH)
        bad_ref[...] = jnp.maximum(bad_ref[...], jnp.max(marks, axis=0))
        if tile % 2:
            done = pl.ds((tile - 1) * TILE, 2 * TILE)
            results.append(
                pltpu.make_async_copy(out_ref.at[done], out_hbm.at[done], e_sem.at[tile // 2])
            )
            results[-1].start()

    for kv in range(2):
        keep_own(kv).wait()
        for t in range(8):
            keep_round(kv, t).wait()
    for i in range(1, 8):
        pltpu.make_async_copy(picked.at[i], picked.at[i], c_send.at[i]).wait()
    for copy in results:
        copy.wait()


def fused(query_rows, key_rows, value_rows, selection):
    dma = pltpu.SemaphoreType.DMA
    anywhere = pl.BlockSpec(memory_space=pl.ANY)
    bf16 = jnp.bfloat16
    return pl.pallas_call(
        fused_kernel,
        out_shape=(
            jax.ShapeDtypeStruct((BLOCK, DH), bf16),
            jax.ShapeDtypeStruct((8, DH), jnp.float32),
            jax.ShapeDtypeStruct((2, BLOCK, DH), bf16),
            jax.ShapeDtypeStruct((2, 8, 4, 2, 64, DH), bf16),
        ),
        in_specs=[anywhere] * 4,
        out_specs=(
            anywhere,
            pl.BlockSpec(memory_space=pltpu.VMEM),
            anywhere,
            anywhere,
        ),
        scratch_shapes=[pltpu.VMEM((8, 64, DH), bf16)] * 16 + [
            pltpu.SMEM((SLOTS, 16), jnp.int32),
            pltpu.VMEM((BLOCK, DH), bf16),
            pltpu.VMEM((64, 4 * DH), bf16),
            pltpu.VMEM((64, 4 * DH), bf16),
            pltpu.VMEM((BLOCK, DH), bf16),
            pltpu.VMEM((8, 8, 2, 64, DH), bf16),
            pltpu.VMEM((2, 4, 512, DH), bf16),
            pltpu.VMEM((2, 8, 4, 2, 64, DH), bf16),
            pltpu.VMEM((2, BLOCK, DH), bf16),
            pltpu.VMEM((BLOCK, 2 * DH), jnp.float32),
            dma((4,)), dma((2, 9)), dma((4,)),
            dma((2, 4, 2)), dma((8, 2)),
            dma((8,)), dma((8, PARTS)), dma((8,)), dma((8, PARTS)),
            dma((7,)), dma((7,)), dma((8,)), dma((8, 8)),
            pltpu.SemaphoreType.REGULAR,
        ],
        compiler_params=pltpu.CompilerParams(
            collective_id=0, has_side_effects=True, vmem_limit_bytes=60 * 2**20
        ),
        name="block_attention",
    )(selection.T, query_rows, key_rows, value_rows)


def finish_kernel(
    fast_ref, bad_ref, sel_hbm, q_hbm, own_hbm, kv_hbm, out_ref, sel_ref, q_ref, own, kv, acc, sem
):
    ctx = lax.axis_index("ctx")
    step = pl.program_id(0)
    size = fast_ref.shape[0]
    marked = jnp.max(bad_ref[...]) > 0.0

    @pl.when(jnp.logical_not(marked))
    def _():
        out_ref[...] = fast_ref[...]

    @pl.when(jnp.logical_and(marked, step == 0))
    def _():
        pairs = ((sel_hbm, sel_ref), (q_hbm, q_ref), (own_hbm, own), (kv_hbm, kv))
        copies = [pltpu.make_async_copy(a, b, sem.at[i]) for i, (a, b) in enumerate(pairs)]
        for copy in copies:
            copy.start()
        for copy in copies:
            copy.wait()

    @pl.when(marked)
    def _():
        q = q_ref[pl.ds(pl.multiple_of(step * size, size), size)]
        acc[...] = jnp.zeros_like(acc)

        def absorb(keys, values, allowed, peak):
            scores = lax.dot_general(
                q, keys, (((1,), (1,)), ((), ())), preferred_element_type=jnp.float32
            )
            scores = jnp.where(allowed, scores, -1e30)
            top = jnp.maximum(peak, jnp.max(scores, axis=1, keepdims=True))
            weights = jnp.where(allowed, jnp.exp2((scores - top[:, :1]) * FACTOR), 0.0)
            before = jnp.exp2((peak - top) * FACTOR)[:, :1]
            wide = jnp.concatenate([values, jnp.ones_like(values)], axis=1)
            acc[...] = acc[...] * before + jnp.dot(
                weights.astype(jnp.bfloat16), wide, preferred_element_type=jnp.float32
            )
            return top

        row_ids = lax.broadcasted_iota(jnp.int32, (size, 512), 0) + step * size
        col_ids = lax.broadcasted_iota(jnp.int32, (size, 512), 1)

        def own_part(i, peak):
            there = pl.ds(pl.multiple_of(i * 512, 512), 512)
            return absorb(own[0, there], own[1, there], col_ids + i * 512 <= row_ids, peak)

        def round_part(t, peak):
            live = jnp.where(col_ids // 64 % 2 == 0, sel_ref[1, ctx], sel_ref[2, ctx]) >= 0
            return absorb(kv[0, t].reshape(512, DH), kv[1, t].reshape(512, DH), live, peak)

        peak = jnp.full((size, DH), -1e30, jnp.float32)
        peak = lax.fori_loop(0, (step + 1) * size // 512, own_part, peak)
        lax.fori_loop(0, 8, round_part, peak)
        out_ref[...] = (acc[:, :DH] / acc[:, DH:]).astype(out_ref.dtype)


def attention(query_rows, key_rows, value_rows, selection):
    fast, bad, own, kv = fused(query_rows, key_rows, value_rows, selection)
    anywhere = pl.BlockSpec(memory_space=pl.ANY)
    size = 1024
    return pl.pallas_call(
        finish_kernel,
        out_shape=jax.ShapeDtypeStruct(fast.shape, fast.dtype),
        grid=(BLOCK // size,),
        in_specs=[
            pl.BlockSpec((size, DH), lambda i: (i, 0)),
            pl.BlockSpec((8, DH), lambda i: (0, 0)),
            anywhere, anywhere, anywhere, anywhere,
        ],
        out_specs=pl.BlockSpec((size, DH), lambda i: (i, 0)),
        scratch_shapes=[
            pltpu.SMEM((SLOTS, 16), jnp.int32),
            pltpu.VMEM((BLOCK, DH), jnp.bfloat16),
            pltpu.VMEM((2, BLOCK, DH), jnp.bfloat16),
            pltpu.VMEM((2, 8, 4, 2, 64, DH), jnp.bfloat16),
            pltpu.VMEM((size, 2 * DH), jnp.float32),
            pltpu.SemaphoreType.DMA((4,)),
        ],
        compiler_params=pltpu.CompilerParams(vmem_limit_bytes=60 * 2**20),
        name="finish",
    )(fast, bad, selection.T, query_rows, own, kv)


def solution(mesh):
    placed = (P("ctx", "head"), P(("ctx", "head"), None), P(("ctx", "head"), None), P())
    return jax.shard_map(
        attention, mesh=mesh, in_specs=placed, out_specs=P("ctx", "head"), check_vma=False
    )
```
